256 devices in a mesh: batch: 8 (over z), proto: 32 (over x, y, core).
Axes of the slice: x: 4, y: 4, z: 8, core: 2. Of those that a mesh axis runs over, the one named last changes fastest.
Arguments:
- teacher_feat: bfloat16 [2048, 256], P('batch'), may hold values from -16 to 16
- student_feat: bfloat16 [8192, 256], P('batch'), may hold values from -16 to 16
- head_weight: bfloat16 [256, 131072], P(None, 'proto'), may hold values from -0.25 to 0.25
- pairing: int32 [8192], P('batch'), may hold values from 0 to 2047, as said below
Outputs:
- loss: float32 [], replicated
- d_student: float32 [8192, 256], P(('batch', 'proto'))
- d_weight: float32 [256, 131072], P('batch', 'proto')
The draws below stay inside these ranges and needn't reach their ends.
Inputs may be any that keep to these rules, and one draw needn't show every extreme that they name: Student row j is paired with a teacher row of its own batch block: pairing[j] // 256 == j // 1024; each teacher row is named by exactly 4 student rows.
All inputs are finite; a program needn't handle non-finite values.
Results may differ from the reference program's by a relative error of at most 0.0045.
Values sent between devices are 32-bit elements; how exact they have to be, the bound alone decides.
No kernel may reach another device: no remote copies, remote signals or barrier semaphores. Data moves between devices by JAX's collectives and lax.ppermute only.
A program may use at most 128 MiB of HBM per device.

```python
import jax
import jax.numpy as jnp
from jax import lax

BN = 256
K = 131072
ITERS = 3
TT = 256
SS = 1024
NT = 2048
NS = 8192


def head_columns(key):
    return jnp.clip(jax.random.normal(key, (BN, K), jnp.float32) / 16.0, -0.25, 0.25)


def feature_rows(key, count_rows):
    feats = jnp.clip(jax.random.normal(key, (count_rows, BN), jnp.float32), -5.0, 5.0)
    return jnp.clip(feats, -16.0, 16.0)


def teacher_rows(key):
    return feature_rows(jax.random.fold_in(key, 1), NT)


def pair_rows(key):
    key = jax.random.fold_in(key, 4)
    groups = NS // SS
    keys = jax.random.split(key, groups)
    orders = jax.vmap(lambda single: jax.random.permutation(single, SS))(keys) % TT
    offsets = jnp.arange(groups, dtype=jnp.int32) * TT
    return (orders.astype(jnp.int32) + offsets[:, None]).reshape(NS).astype(jnp.int32)


def draw_head_weight(key, part):
    return head_columns(key).astype(jnp.bfloat16)


def draw_teacher_feat(key, part):
    return teacher_rows(key).astype(jnp.bfloat16)


def draw_student_feat(key, part):
    teacher = teacher_rows(key)
    pairs = pair_rows(key)
    key = jax.random.fold_in(key, 2)
    copied = jnp.take(teacher, pairs, axis=0)
    noise = jnp.clip(jax.random.normal(key, (NS, BN), jnp.float32), -5.0, 5.0)
    feats = copied + 0.3 * noise
    return jnp.clip(feats, -16.0, 16.0).astype(jnp.bfloat16)


def draw_pairing(key, part):
    return pair_rows(key)


def setup_inputs(seed: int = 0) -> dict:
    splits = jax.random.split(jax.random.key(seed), 5)
    return {
        "teacher_feat": draw_teacher_feat(jax.random.fold_in(splits[4], 71), 0),
        "student_feat": draw_student_feat(jax.random.fold_in(splits[4], 71), 0),
        "head_weight": draw_head_weight(jax.random.fold_in(splits[4], 71), 0),
        "pairing": draw_pairing(jax.random.fold_in(splits[4], 71), 0),
    }


teacher_temp = 0.07
student_temp = 0.1


def reference(teacher_feat, student_feat, head_weight, pairing):
    total_t = teacher_feat.shape[0]
    total_s = student_feat.shape[0]
    span = min(K, 4096)
    blocks_count = K // span
    weight_blocks = head_weight.reshape(BN, blocks_count, span).transpose(1, 0, 2)

    def teacher_scores(columns):
        return jnp.dot(teacher_feat, columns, preferred_element_type=jnp.float32) / teacher_temp

    teacher_high = jnp.max(lax.map(lambda columns: jnp.max(teacher_scores(columns), axis=1), weight_blocks), axis=0)

    def expo_of(columns):
        return jnp.exp(teacher_scores(columns) - teacher_high[:, None])

    row_scale = jnp.ones((total_t,), jnp.float32)
    column_scale = jnp.ones((blocks_count, span), jnp.float32)
    for iteration in range(ITERS):
        current = row_scale
        column_scale = lax.map(lambda columns: 1.0 / (K * jnp.sum(expo_of(columns) * current[:, None], axis=0)), weight_blocks)
        sample_total = jnp.sum(lax.map(lambda both: jnp.sum(expo_of(both[0]) * both[1][None, :], axis=1), (weight_blocks, column_scale)), axis=0)
        row_scale = 1.0 / (total_t * sample_total)
    column_flat = column_scale.reshape(K)

    block_rows = min(512, total_s)
    steps_count = total_s // block_rows
    feats = student_feat.reshape(steps_count, block_rows, BN)
    pairs = pairing.reshape(steps_count, block_rows)

    def advance(carry, item):
        loss_sum, weight_grad = carry
        block_feat, block_pair = item
        scores = jnp.dot(block_feat, head_weight, preferred_element_type=jnp.float32) / student_temp
        row_high = jnp.max(scores, axis=1)
        lse_rows = row_high + jnp.log(jnp.sum(jnp.exp(scores - row_high[:, None]), axis=1))
        prob = jnp.exp(scores - lse_rows[:, None])
        teach = jnp.dot(jnp.take(teacher_feat, block_pair, axis=0), head_weight, preferred_element_type=jnp.float32) / teacher_temp
        expo = jnp.exp(teach - jnp.take(teacher_high, block_pair)[:, None])
        wanted = total_t * jnp.take(row_scale, block_pair)[:, None] * expo * column_flat[None, :]
        loss_sum = loss_sum + jnp.sum(wanted * (lse_rows[:, None] - scores))
        gradient = ((prob - wanted) / student_temp).astype(jnp.bfloat16)
        d_rows = jnp.dot(gradient, head_weight.T, preferred_element_type=jnp.float32)
        weight_grad = weight_grad + jnp.dot(block_feat.T, gradient, preferred_element_type=jnp.float32)
        return (loss_sum, weight_grad), d_rows

    start = (jnp.zeros((), jnp.float32), jnp.zeros((BN, K), jnp.float32))
    (loss_sum, weight_grad), d_rows = lax.scan(advance, start, (feats, pairs))
    return loss_sum / total_s, d_rows.reshape(total_s, BN), weight_grad
```

```python
import math

import jax
import jax.numpy as jnp
from jax import lax
from jax.experimental import pallas as pl
from jax.experimental.pallas import tpu as pltpu
from jax.sharding import PartitionSpec as P

ITERS = 3
LANES = 128
CHUNK = 512
TEACHER_TEMP = 0.07
STUDENT_TEMP = 0.1
LOG2E = math.log2(math.e)
T_SCALE = LOG2E / TEACHER_TEMP
S_SCALE = LOG2E / STUDENT_TEMP
F32 = jnp.float32
BF16 = jnp.bfloat16
NN = (((1,), (0,)), ((), ()))
NT = (((1,), (1,)), ((), ()))
TN = (((0,), (0,)), ((), ()))
VMEM_LIMIT = 48 * 1024 * 1024


def mm(a, b, dims):
    return lax.dot_general(a, b, dims, preferred_element_type=F32)


def halves(x):
    high = x.astype(BF16)
    return high, (x - high.astype(F32)).astype(BF16)


def by_sublane(x, combine):
    return combine(x.reshape(x.shape[0] // 8, 8, x.shape[1]), axis=0)


def whole(shape):
    return pl.BlockSpec(shape, lambda c: (0,) * len(shape))


def call(body, grid, in_specs, out_specs, out_shape, scratch, flops, transcendentals, size):
    return pl.pallas_call(
        body,
        grid=(grid,),
        in_specs=in_specs,
        out_specs=out_specs,
        out_shape=out_shape,
        scratch_shapes=scratch,
        cost_estimate=pl.CostEstimate(
            flops=flops, transcendentals=transcendentals, bytes_accessed=size
        ),
        compiler_params=pltpu.CompilerParams(
            dimension_semantics=("arbitrary",), vmem_limit_bytes=VMEM_LIMIT
        ),
    )


def struct(shape, dtype=F32):
    return jax.ShapeDtypeStruct(shape, dtype)


def put_rows(ref, first, row):
    for i in range(row.shape[1] // LANES):
        ref[first + i : first + i + 1, :] = row[:, i * LANES : (i + 1) * LANES]


def student_stats(sf, tf, w, onehot, peers):
    rows, width = sf.shape
    t_rows = tf.shape[0]
    columns = w.shape[1]
    steps = columns // CHUNK
    s_rows, tr = rows // LANES, t_rows // LANES
    lines = -(-(2 * s_rows + tr) // 8) * 8

    def body(sf_ref, tf_ref, w_ref, oh_ref, wt_ref, gt_ref, out_ref, high, total, t_high, line):
        step = pl.program_id(0)

        @pl.when(step == 0)
        def _():
            high[...] = jnp.full_like(high, -3e38)
            total[...] = jnp.zeros_like(total)
            t_high[...] = jnp.full_like(t_high, -3e38)
            gt_ref[...] = mm(sf_ref[...], oh_ref[...], TN)

        wt = w_ref[...].T
        wt_ref[...] = wt
        scores = mm(wt, sf_ref[...], NT)
        before = high[...]
        now = jnp.maximum(before, by_sublane(scores, jnp.max))
        high[...] = now
        groups = scores.reshape(CHUNK // 8, 8, rows)
        part = jnp.sum(jnp.exp2((groups - now[None]) * S_SCALE), axis=0)
        total[...] = total[...] * jnp.exp2((before - now) * S_SCALE) + part
        t_high[...] = jnp.maximum(t_high[...], by_sublane(mm(wt, tf_ref[...], NT), jnp.max))

        @pl.when(step == steps - 1)
        def _():
            best = jnp.max(high[...], axis=0, keepdims=True)
            summed = jnp.sum(
                total[...] * jnp.exp2((high[...] - best) * S_SCALE), axis=0, keepdims=True
            )
            line[...] = jnp.zeros_like(line)
            put_rows(line, 0, best)
            put_rows(line, s_rows, summed)
            put_rows(line, 2 * s_rows, jnp.max(t_high[...], axis=0, keepdims=True))
            out_ref[...] = jnp.broadcast_to(line[...][None], out_ref.shape)

    return call(
        body,
        steps,
        [
            whole(sf.shape),
            whole(tf.shape),
            pl.BlockSpec((width, CHUNK), lambda c: (0, c)),
            whole(onehot.shape),
        ],
        [
            pl.BlockSpec((CHUNK, width), lambda c: (c, 0)),
            whole((width, t_rows)),
            whole((peers, lines, LANES)),
        ],
        [
            struct((columns, width), BF16),
            struct((width, t_rows)),
            struct((peers, lines, LANES)),
        ],
        [
            pltpu.VMEM((8, rows), F32),
            pltpu.VMEM((8, rows), F32),
            pltpu.VMEM((8, t_rows), F32),
            pltpu.VMEM((lines, LANES), F32),
        ],
        2 * columns * width * (rows + t_rows),
        columns * rows,
        8 * 2**20,
    )(sf, tf, w, onehot)


def merge_stats(stats, gt, rows, batches):
    width, t_rows = gt.shape
    share = width // batches
    s_rows, tr = rows // LANES, t_rows // LANES

    def body(stats_ref, gt_ref, lse_ref, out_ref):
        highs = stats_ref[:, :s_rows, :]
        best = jnp.max(highs, axis=0)
        total = jnp.sum(
            stats_ref[:, s_rows : 2 * s_rows, :] * jnp.exp2((highs - best[None]) * S_SCALE), axis=0
        )
        lse_ref[...] = best * S_SCALE + jnp.log2(total)
        t_best = jnp.max(stats_ref[:, 2 * s_rows : 2 * s_rows + tr, :], axis=0) * T_SCALE
        row = jnp.concatenate([t_best[i : i + 1, :] for i in range(tr)], axis=1)
        for b in range(batches):
            out_ref[b, :share, :] = gt_ref[b * share : (b + 1) * share, :]
            out_ref[b, share:, :] = jnp.broadcast_to(row, (8, t_rows))

    return call(
        body,
        1,
        [whole(stats.shape), whole(gt.shape)],
        [whole((s_rows, LANES)), whole((batches, share + 8, t_rows))],
        [struct((s_rows, LANES)), struct((batches, share + 8, t_rows))],
        [],
        stats.size * 4,
        stats.size,
        2**21,
    )(stats, gt)


def student_grads(sf, w, wt, lse, peers):
    rows, width = sf.shape
    columns = w.shape[1]
    steps = columns // CHUNK
    s_rows = rows // LANES

    def body(sf_ref, w_ref, wt_ref, lse_ref, ds_ref, dw_ref, lse_row, sft, acc):
        step = pl.program_id(0)

        @pl.when(step == 0)
        def _():
            for i in range(s_rows):
                lse_row[:, i * LANES : (i + 1) * LANES] = lse_ref[i : i + 1, :]
            sft[...] = sf_ref[...].T
            acc[...] = jnp.zeros_like(acc)

        scores = mm(wt_ref[...], sf_ref[...], NT)
        high, low = halves(jnp.exp2(scores * S_SCALE - lse_row[...]))
        acc[...] += mm(w_ref[...], high, NN) + mm(w_ref[...], low, NN)
        dw_ref[...] = (mm(sft[...], high, NT) + mm(sft[...], low, NT)) / STUDENT_TEMP

        @pl.when(step == steps - 1)
        def _():
            ds_ref[...] = (acc[...].T / STUDENT_TEMP).reshape(ds_ref.shape)

    return call(
        body,
        steps,
        [
            whole(sf.shape),
            pl.BlockSpec((width, CHUNK), lambda c: (0, c)),
            pl.BlockSpec((CHUNK, width), lambda c: (c, 0)),
            whole(lse.shape),
        ],
        [
            whole((peers, rows // peers, width)),
            pl.BlockSpec((width, CHUNK), lambda c: (0, c)),
        ],
        [struct((peers, rows // peers, width)), struct((width, columns))],
        [
            pltpu.VMEM((1, rows), F32),
            pltpu.VMEM((width, rows), BF16),
            pltpu.VMEM((width, rows), F32),
        ],
        10 * columns * width * rows,
        columns * rows,
        10 * 2**20,
    )(sf, w, wt, lse)


def fill_offsets(offset, packed, blocks, per_block):
    for i in range(blocks):
        for j in range(per_block):
            line = i * per_block + j
            offset[i : i + 1, j * LANES : (j + 1) * LANES] = packed[line : line + 1, :]


def expos_and_scale(wt, feats, offset, expo, blocks, all_columns):
    partial = None
    for i in range(blocks):
        scores = mm(wt, feats[i], NN)
        values = jnp.exp2(scores * T_SCALE - offset[i : i + 1, :])
        expo[i] = values
        for j in range(values.shape[1] // LANES):
            piece = values[:, j * LANES : (j + 1) * LANES]
            partial = piece if partial is None else partial + piece
    return 1.0 / (all_columns * jnp.sum(partial, axis=1, keepdims=True))


def add_rows(expo, scale, mass, blocks):
    for i in range(blocks):
        mass[i] += by_sublane(expo[i] * scale, jnp.sum)


def put_mass(mass, line, blocks):
    for i in range(blocks):
        row = jnp.sum(mass[i], axis=0, keepdims=True)
        put_rows(line, i * (row.shape[1] // LANES), row)


def first_iteration(feats_f32, shared, wt, peers):
    blocks, width, t_rows = feats_f32.shape
    columns = wt.shape[0]
    steps = columns // CHUNK
    tr = t_rows // LANES
    share = shared.shape[1] - 8

    def body(feat_ref, shared_ref, wt_ref, feat_out, off_out, out_ref, offset, expo, mass, line):
        step = pl.program_id(0)

        @pl.when(step == 0)
        def _():
            feat_out[...] = feat_ref[...].astype(BF16)
            for i in range(blocks):
                row = shared_ref[i, share : share + 1, :]
                offset[i : i + 1, :] = row
                put_rows(off_out, i * tr, row)
            mass[...] = jnp.zeros_like(mass)

        scale = expos_and_scale(wt_ref[...], feat_out, offset, expo, blocks, columns * peers)
        add_rows(expo, scale, mass, blocks)

        @pl.when(step == steps - 1)
        def _():
            put_mass(mass, line, blocks)
            out_ref[...] = jnp.broadcast_to(line[...][None], out_ref.shape)

    return call(
        body,
        steps,
        [
            whole(feats_f32.shape),
            whole(shared.shape),
            pl.BlockSpec((CHUNK, width), lambda c: (c, 0)),
        ],
        [
            whole(feats_f32.shape),
            whole((blocks * tr, LANES)),
            whole((peers, blocks * tr, LANES)),
        ],
        [
            struct(feats_f32.shape, BF16),
            struct((blocks * tr, LANES)),
            struct((peers, blocks * tr, LANES)),
        ],
        [
            pltpu.VMEM((max(blocks, 8), t_rows), F32),
            pltpu.VMEM((blocks, CHUNK, t_rows), F32),
            pltpu.VMEM((blocks, 8, t_rows), F32),
            pltpu.VMEM((blocks * tr, LANES), F32),
        ],
        2 * columns * width * t_rows * blocks,
        columns * t_rows * blocks,
        5 * 2**20,
    )(feats_f32, shared, wt)


def next_iteration(feats, old, received, wt):
    blocks, width, t_rows = feats.shape
    columns = wt.shape[0]
    peers = received.shape[0]
    steps = columns // CHUNK
    tr = t_rows // LANES
    total_t = blocks * t_rows

    def body(feat_ref, old_ref, recv_ref, wt_ref, off_out, out_ref, offset, expo, mass, line):
        step = pl.program_id(0)

        @pl.when(step == 0)
        def _():
            packed = old_ref[...] + jnp.log2(total_t * jnp.sum(recv_ref[...], axis=0))
            off_out[...] = packed
            fill_offsets(offset, packed, blocks, tr)
            mass[...] = jnp.zeros_like(mass)

        scale = expos_and_scale(wt_ref[...], feat_ref, offset, expo, blocks, columns * peers)
        add_rows(expo, scale, mass, blocks)

        @pl.when(step == steps - 1)
        def _():
            put_mass(mass, line, blocks)
            out_ref[...] = jnp.broadcast_to(line[...][None], out_ref.shape)

    return call(
        body,
        steps,
        [
            whole(feats.shape),
            whole(old.shape),
            whole(received.shape),
            pl.BlockSpec((CHUNK, width), lambda c: (c, 0)),
        ],
        [whole(old.shape), whole((peers, blocks * tr, LANES))],
        [struct(old.shape), struct((peers, blocks * tr, LANES))],
        [
            pltpu.VMEM((max(blocks, 8), t_rows), F32),
            pltpu.VMEM((blocks, CHUNK, t_rows), F32),
            pltpu.VMEM((blocks, 8, t_rows), F32),
            pltpu.VMEM((blocks * tr, LANES), F32),
        ],
        2 * columns * width * t_rows * blocks,
        columns * t_rows * blocks,
        4 * 2**20,
    )(feats, old, received, wt)


def last_iteration(me, feats, old, received, w, wt, gt, onehot):
    blocks, width, t_rows = feats.shape
    columns = wt.shape[0]
    peers = received.shape[0]
    steps = columns // CHUNK
    tr = t_rows // LANES
    total_t = blocks * t_rows
    rows = onehot.shape[0]
    lines = -(-(blocks * tr + tr) // 8) * 8

    def body(
        me_ref, feat_ref, old_ref, recv_ref, w_ref, wt_ref, gt_ref, oh_ref,
        off_out, scale_out, taught_ref, out_ref, offset, expo, mass, line, acc,
    ):
        step = pl.program_id(0)

        @pl.when(step == 0)
        def _():
            packed = old_ref[...] + jnp.log2(total_t * jnp.sum(recv_ref[...], axis=0))
            off_out[...] = packed
            fill_offsets(offset, packed, blocks, tr)
            mass[...] = jnp.zeros_like(mass)
            acc[...] = jnp.zeros_like(acc)

        scale = expos_and_scale(wt_ref[...], feat_ref, offset, expo, blocks, columns * peers)
        scale_out[...] = jnp.broadcast_to(scale, scale_out.shape)
        add_rows(expo, scale, mass, blocks)
        high, low = halves(expo[me_ref[0]] * scale)
        acc[...] += mm(w_ref[...], high, NN) + mm(w_ref[...], low, NN)

        @pl.when(step == steps - 1)
        def _():
            line[...] = jnp.zeros_like(line)
            put_mass(mass, line, blocks)
            put_rows(line, blocks * tr, jnp.sum(acc[...] * gt_ref[...], axis=0, keepdims=True))
            out_ref[...] = jnp.broadcast_to(line[...][None], out_ref.shape)
            high, low = halves(acc[...])
            taught = mm(oh_ref[...], high, NT) + mm(oh_ref[...], low, NT)
            taught_ref[...] = taught.reshape(taught_ref.shape)

    return call(
        body,
        steps,
        [
            pl.BlockSpec(memory_space=pltpu.SMEM),
            whole(feats.shape),
            whole(old.shape),
            whole(received.shape),
            pl.BlockSpec((width, CHUNK), lambda c: (0, c)),
            pl.BlockSpec((CHUNK, width), lambda c: (c, 0)),
            whole(gt.shape),
            whole(onehot.shape),
        ],
        [
            whole(old.shape),
            pl.BlockSpec((CHUNK, LANES), lambda c: (c, 0)),
            whole((peers, rows // peers, width)),
            whole((peers, lines, LANES)),
        ],
        [
            struct(old.shape),
            struct((columns, LANES)),
            struct((peers, rows // peers, width)),
            struct((peers, lines, LANES)),
        ],
        [
            pltpu.VMEM((max(blocks, 8), t_rows), F32),
            pltpu.VMEM((blocks, CHUNK, t_rows), F32),
            pltpu.VMEM((blocks, 8, t_rows), F32),
            pltpu.VMEM((lines, LANES), F32),
            pltpu.VMEM((width, t_rows), F32),
        ],
        2 * columns * width * t_rows * (blocks + 2),
        columns * t_rows * blocks,
        8 * 2**20,
    )(me, feats, old, received, w, wt, gt, onehot)


def block_loss(me, received, lse, blocks):
    peers, lines, _ = received.shape
    tr = 2
    for_rows = lse.shape

    def body(me_ref, recv_ref, lse_ref, out_ref, log_ref, inv_ref):
        total = jnp.sum(recv_ref[...], axis=0)
        n = log_ref.shape[0]
        log_ref[...] = jnp.log2(total[:n])
        start = me_ref[0] * inv_ref.shape[0]
        mine = jnp.sum(recv_ref[:, pl.ds(start, inv_ref.shape[0]), :], axis=0)
        inverse = 1.0 / mine
        inv_ref[...] = inverse
        product = jnp.sum(total[n : n + inv_ref.shape[0]] * inverse) / STUDENT_TEMP
        part = jnp.sum(lse_ref[...]) / LOG2E - product
        out_ref[...] = jnp.full(out_ref.shape, part, F32)

    return call(
        body,
        1,
        [
            pl.BlockSpec(memory_space=pltpu.SMEM),
            whole(received.shape),
            whole(for_rows),
        ],
        [whole((blocks, 8, LANES)), whole((blocks * tr, LANES)), whole((tr, LANES))],
        [struct((blocks, 8, LANES)), struct((blocks * tr, LANES)), struct((tr, LANES))],
        [],
        received.size,
        1024,
        2**19,
    )(me, received, lse)


def weight_grad(feats, old, log_mass, wt, shared, scale, prob_part):
    blocks, width, t_rows = feats.shape
    columns = wt.shape[0]
    steps = columns // CHUNK
    tr = t_rows // LANES
    share = shared.shape[1] - 8

    def body(feat_ref, old_ref, log_ref, wt_ref, sh_ref, scale_ref, prob_ref, out_ref, offset, g):
        step = pl.program_id(0)

        @pl.when(step == 0)
        def _():
            fill_offsets(offset, old_ref[...] + log_ref[...], blocks, tr)
            for i in range(blocks):
                high, low = halves(sh_ref[i, :share, :])
                g[i] = jnp.concatenate([high, low, jnp.zeros((LANES - 2 * share, t_rows), BF16)])

        acc = jnp.zeros((CHUNK, LANES), F32)
        for i in range(blocks):
            scores = mm(wt_ref[...], feat_ref[i], NN)
            high, low = halves(jnp.exp2(scores * T_SCALE - offset[i : i + 1, :]))
            acc += mm(high, g[i], NT) + mm(low, g[i], NT)
        turned = (acc * scale_ref[...]).T
        taught = turned[:share] + turned[share : 2 * share]
        out_ref[...] = prob_ref[...] - taught / STUDENT_TEMP

    return call(
        body,
        steps,
        [
            whole(feats.shape),
            whole(old.shape),
            whole(log_mass.shape),
            pl.BlockSpec((CHUNK, width), lambda c: (c, 0)),
            whole(shared.shape),
            pl.BlockSpec((CHUNK, LANES), lambda c: (c, 0)),
            pl.BlockSpec((share, CHUNK), lambda c: (0, c)),
        ],
        [pl.BlockSpec((share, CHUNK), lambda c: (0, c))],
        [struct((share, columns))],
        [
            pltpu.VMEM((max(blocks, 8), t_rows), F32),
            pltpu.VMEM((blocks, LANES, t_rows), BF16),
        ],
        2 * columns * width * t_rows * blocks * 3,
        columns * t_rows * blocks,
        6 * 2**20,
    )(feats, old, log_mass, wt, shared, scale, prob_part)[0]


def student_grad(prob_parts, taught_parts, inverse, picks):
    _, rows, width = prob_parts.shape
    tr = inverse.shape[0]

    def body(prob_ref, taught_ref, inv_ref, pick_ref, out_ref):
        row = jnp.concatenate([inv_ref[i : i + 1, :] for i in range(tr)], axis=1)
        factor = jnp.sum(pick_ref[...] * row, axis=1, keepdims=True) / STUDENT_TEMP
        out_ref[...] = jnp.sum(prob_ref[...], axis=0) - jnp.sum(taught_ref[...], axis=0) * factor

    return call(
        body,
        1,
        [
            whole(prob_parts.shape),
            whole(taught_parts.shape),
            whole(inverse.shape),
            whole(picks.shape),
        ],
        [whole((rows, width))],
        [struct((rows, width))],
        [],
        prob_parts.size * 2,
        0,
        prob_parts.size * 8,
    )(prob_parts, taught_parts, inverse, picks)[0]


def per_device(tf, sf, w, pairing):
    t_rows = tf.shape[0]
    rows = sf.shape[0]
    blocks = lax.axis_size("batch")
    peers = lax.axis_size("proto")
    me = lax.axis_index("batch")

    def swap(x, axis):
        return lax.all_to_all(x, axis, 0, 0)

    feats_f32 = lax.all_gather(tf.T.astype(F32), "batch")
    pairs = pairing - me * t_rows
    onehot = (pairs[:, None] == jnp.arange(t_rows, dtype=jnp.int32)[None, :]).astype(BF16)
    wt, gt, stats = student_stats(sf, tf, w, onehot, peers)
    stats = swap(stats, "proto")
    lse, shared = merge_stats(stats, gt, rows, blocks)
    shared = swap(shared, "batch")
    ds_prob, dw_prob = student_grads(sf, w, wt, lse, peers)
    dw_prob = lax.psum_scatter(dw_prob, "batch", scatter_dimension=0, tiled=True)
    ds_prob = swap(ds_prob, "proto")

    mine = me.astype(jnp.int32).reshape(1)
    feats, offset, mass = first_iteration(feats_f32, shared, wt, peers)
    for _ in range(ITERS - 2):
        offset, mass = next_iteration(feats, offset, swap(mass, "proto"), wt)
    offset, scale, taught, mass = last_iteration(
        mine, feats, offset, swap(mass, "proto"), w, wt, gt, onehot
    )
    taught = swap(taught, "proto")
    mass = swap(mass, "proto")
    part, log_mass, inverse = block_loss(mine, mass, lse, blocks)
    part = swap(part, "batch")
    d_weight = weight_grad(feats, offset, log_mass, wt, shared, scale, dw_prob)
    each = rows // peers
    picks = lax.dynamic_slice_in_dim(onehot, lax.axis_index("proto") * each, each, 0).astype(F32)
    d_student = student_grad(ds_prob, taught, inverse, picks)
    loss = jnp.sum(part[:, 0, 0]) / (rows * blocks)
    return loss, d_student, d_weight


def solution(mesh):
    placed = (P("batch", None), P("batch", None), P(None, "proto"), P("batch"))
    return jax.shard_map(
        per_device,
        mesh=mesh,
        in_specs=placed,
        out_specs=(P(), P(("batch", "proto"), None), P("batch", "proto")),
        check_vma=False,
    )
```

```python
import math

import jax
import jax.numpy as jnp
from jax import lax
from jax.experimental import pallas as pl
from jax.experimental.pallas import tpu as pltpu
from jax.sharding import PartitionSpec as P

ITERS = 3
LANES = 128
S_CHUNK = 512
T_CHUNK = 1024
TEACHER_TEMP = 0.07
STUDENT_TEMP = 0.1
LOG2E = math.log2(math.e)
T_SCALE = LOG2E / TEACHER_TEMP
S_SCALE = LOG2E / STUDENT_TEMP
F32 = jnp.float32
BF16 = jnp.bfloat16
NN = (((1,), (0,)), ((), ()))
NT = (((1,), (1,)), ((), ()))
TN = (((0,), (0,)), ((), ()))
VMEM_LIMIT = 56 * 1024 * 1024


def mm(a, b, dims):
    return lax.dot_general(a, b, dims, preferred_element_type=F32)


def halves(x):
    high = x.astype(BF16)
    return high, (x - high.astype(F32)).astype(BF16)


def by_sublane(x, combine):
    return combine(x.reshape(x.shape[0] // 8, 8, x.shape[1]), axis=0)


def whole(shape):
    return pl.BlockSpec(shape, lambda c: (0,) * len(shape))


def call(
    body, grid, in_specs, out_specs, out_shape, scratch, flops, transcendentals, size, aliases=None
):
    return pl.pallas_call(
        body,
        grid=(grid,),
        in_specs=in_specs,
        out_specs=out_specs,
        out_shape=out_shape,
        scratch_shapes=scratch,
        input_output_aliases=aliases or {},
        cost_estimate=pl.CostEstimate(
            flops=flops, transcendentals=transcendentals, bytes_accessed=size
        ),
        compiler_params=pltpu.CompilerParams(
            dimension_semantics=("arbitrary",), vmem_limit_bytes=VMEM_LIMIT
        ),
    )


def struct(shape, dtype=F32):
    return jax.ShapeDtypeStruct(shape, dtype)


def put_rows(ref, first, row):
    for i in range(row.shape[1] // LANES):
        ref[first + i : first + i + 1, :] = row[:, i * LANES : (i + 1) * LANES]


def core_half(core, tf):
    t_rows, width = tf.shape
    part = t_rows // 2

    def body(core_ref, tf_ref, out_ref):
        start = pl.multiple_of(core_ref[0] * part, part)
        out_ref[...] = tf_ref[pl.ds(start, part), :].astype(F32).T

    return call(
        body,
        1,
        [pl.BlockSpec(memory_space=pltpu.SMEM), whole(tf.shape)],
        [whole((width, part))],
        [struct((width, part))],
        [],
        0,
        0,
        2**18,
    )(core, tf)[0]


def student_stats(sf, tf, w, onehot, peers):
    rows, width = sf.shape
    t_rows = tf.shape[0]
    columns = w.shape[1]
    steps = columns // S_CHUNK
    s_rows, tr = rows // LANES, t_rows // LANES
    lines = -(-(2 * s_rows + tr) // 8) * 8

    def body(sf_ref, tf_ref, w_ref, oh_ref, wt_ref, gt_ref, out_ref, high, total, t_high, line):
        step = pl.program_id(0)

        @pl.when(step == 0)
        def _():
            high[...] = jnp.full_like(high, -3e38)
            total[...] = jnp.zeros_like(total)
            t_high[...] = jnp.full_like(t_high, -3e38)
            gt_ref[...] = mm(sf_ref[...], oh_ref[...], TN)

        wt = w_ref[...].T
        wt_ref[...] = wt
        scores = mm(wt, sf_ref[...], NT)
        before = high[...]
        now = jnp.maximum(before, by_sublane(scores, jnp.max))
        high[...] = now
        groups = scores.reshape(S_CHUNK // 8, 8, rows)
        part = jnp.sum(jnp.exp2((groups - now[None]) * S_SCALE), axis=0)
        total[...] = total[...] * jnp.exp2((before - now) * S_SCALE) + part
        t_high[...] = jnp.maximum(t_high[...], by_sublane(mm(wt, tf_ref[...], NT), jnp.max))

        @pl.when(step == steps - 1)
        def _():
            best = jnp.max(high[...], axis=0, keepdims=True)
            summed = jnp.sum(
                total[...] * jnp.exp2((high[...] - best) * S_SCALE), axis=0, keepdims=True
            )
            line[...] = jnp.zeros_like(line)
            put_rows(line, 0, best)
            put_rows(line, s_rows, summed)
            put_rows(line, 2 * s_rows, jnp.max(t_high[...], axis=0, keepdims=True))
            out_ref[...] = jnp.broadcast_to(line[...][None], out_ref.shape)

    return call(
        body,
        steps,
        [
            whole(sf.shape),
            whole(tf.shape),
            pl.BlockSpec((width, S_CHUNK), lambda c: (0, c)),
            whole(onehot.shape),
        ],
        [
            pl.BlockSpec((S_CHUNK, width), lambda c: (c, 0)),
            whole((width, t_rows)),
            whole((peers, lines, LANES)),
        ],
        [
            struct((columns, width), BF16),
            struct((width, t_rows)),
            struct((peers, lines, LANES)),
        ],
        [
            pltpu.VMEM((8, rows), F32),
            pltpu.VMEM((8, rows), F32),
            pltpu.VMEM((8, t_rows), F32),
            pltpu.VMEM((lines, LANES), F32),
        ],
        2 * columns * width * (rows + t_rows),
        columns * rows,
        8 * 2**20,
    )(sf, tf, w, onehot)


def merge_stats(stats, gt, rows, batches):
    width, t_rows = gt.shape
    share = width // batches
    s_rows, tr = rows // LANES, t_rows // LANES

    def body(stats_ref, gt_ref, lse_ref, out_ref):
        highs = stats_ref[:, :s_rows, :]
        best = jnp.max(highs, axis=0)
        total = jnp.sum(
            stats_ref[:, s_rows : 2 * s_rows, :] * jnp.exp2((highs - best[None]) * S_SCALE), axis=0
        )
        lse_ref[...] = best * S_SCALE + jnp.log2(total)
        t_best = jnp.max(stats_ref[:, 2 * s_rows : 2 * s_rows + tr, :], axis=0) * T_SCALE
        row = jnp.concatenate([t_best[i : i + 1, :] for i in range(tr)], axis=1)
        for b in range(batches):
            out_ref[b, :share, :] = gt_ref[b * share : (b + 1) * share, :]
            out_ref[b, share:, :] = jnp.broadcast_to(row, (8, t_rows))

    return call(
        body,
        1,
        [whole(stats.shape), whole(gt.shape)],
        [whole((s_rows, LANES)), whole((batches, share + 8, t_rows))],
        [struct((s_rows, LANES)), struct((batches, share + 8, t_rows))],
        [],
        stats.size * 4,
        stats.size,
        2**21,
    )(stats, gt)


def student_grads(sf, w, wt, lse, half, before, peers):
    rows, width = sf.shape
    columns = w.shape[1]
    steps = columns // S_CHUNK // 2
    first = half * steps
    s_rows = rows // LANES

    def body(sf_ref, w_ref, wt_ref, lse_ref, *rest):
        if half:
            _, old_ref, ds_ref, dw_ref, lse_row, sft, acc = rest
        else:
            ds_ref, dw_ref, lse_row, sft, acc = rest
        step = pl.program_id(0)

        @pl.when(step == 0)
        def _():
            for i in range(s_rows):
                lse_row[:, i * LANES : (i + 1) * LANES] = lse_ref[i : i + 1, :]
            sft[...] = sf_ref[...].T
            acc[...] = old_ref[...] if half else jnp.zeros_like(acc)

        scores = mm(wt_ref[...], sf_ref[...], NT)
        high, low = halves(jnp.exp2(scores * S_SCALE - lse_row[...]))
        acc[...] += mm(w_ref[...], high, NN) + mm(w_ref[...], low, NN)
        dw_ref[...] = (mm(sft[...], high, NT) + mm(sft[...], low, NT)) / STUDENT_TEMP

        @pl.when(step == steps - 1)
        def _():
            if half:
                ds_ref[...] = (acc[...].T / STUDENT_TEMP).reshape(ds_ref.shape)
            else:
                ds_ref[...] = acc[...]

    ds_shape = (peers, rows // peers, width) if half else (width, rows)
    in_specs = [
        whole(sf.shape),
        pl.BlockSpec((width, S_CHUNK), lambda c: (0, c + first)),
        pl.BlockSpec((S_CHUNK, width), lambda c: (c + first, 0)),
        whole(lse.shape),
    ]
    operands = [sf, w, wt, lse]
    if half:
        in_specs += [pl.BlockSpec(memory_space=pl.ANY), whole((width, rows))]
        operands += [before[1], before[0]]
    return call(
        body,
        steps,
        in_specs,
        [whole(ds_shape), pl.BlockSpec((width, S_CHUNK), lambda c: (0, c + first))],
        [struct(ds_shape), struct((width, columns))],
        [
            pltpu.VMEM((1, rows), F32),
            pltpu.VMEM((width, rows), BF16),
            pltpu.VMEM((width, rows), F32),
        ],
        5 * columns * width * rows,
        columns * rows // 2,
        6 * 2**20,
        {4: 1} if half else None,
    )(*operands)


def fill_offsets(offset, packed, blocks, per_block):
    for i in range(blocks):
        for j in range(per_block):
            line = i * per_block + j
            offset[i : i + 1, j * LANES : (j + 1) * LANES] = packed[line : line + 1, :]


def expos_and_scale(wt, feats, offset, expo, blocks, all_columns):
    partial = None
    for i in range(blocks):
        scores = mm(wt, feats[i], NN)
        values = jnp.exp2(scores * T_SCALE - offset[i : i + 1, :])
        expo[i] = values
        for j in range(values.shape[1] // LANES):
            piece = values[:, j * LANES : (j + 1) * LANES]
            partial = piece if partial is None else partial + piece
    return 1.0 / (all_columns * jnp.sum(partial, axis=1, keepdims=True))


def add_rows(expo, scale, mass, blocks):
    for i in range(blocks):
        mass[i] += by_sublane(expo[i] * scale, jnp.sum)


def put_mass(mass, line, blocks):
    for i in range(blocks):
        row = jnp.sum(mass[i], axis=0, keepdims=True)
        put_rows(line, i * (row.shape[1] // LANES), row)


def first_iteration(core, own_half, other_half, shared, wt, peers):
    blocks, width, part = own_half.shape
    t_rows = 2 * part
    full = (blocks, width, t_rows)
    columns = wt.shape[0]
    steps = columns // T_CHUNK
    tr = t_rows // LANES
    share = shared.shape[1] - 8

    def body(
        core_ref, own_ref, other_ref, shared_ref, wt_ref,
        feat_out, off_out, out_ref, offset, expo, mass, line,
    ):
        step = pl.program_id(0)

        @pl.when(step == 0)
        def _():
            core = core_ref[0]
            feat_out[:, :, pl.ds(pl.multiple_of(core * part, part), part)] = own_ref[...].astype(BF16)
            feat_out[:, :, pl.ds(pl.multiple_of((1 - core) * part, part), part)] = other_ref[
                ...
            ].astype(BF16)
            for i in range(blocks):
                row = shared_ref[i, share : share + 1, :]
                offset[i : i + 1, :] = row
                put_rows(off_out, i * tr, row)
            mass[...] = jnp.zeros_like(mass)

        scale = expos_and_scale(wt_ref[...], feat_out, offset, expo, blocks, columns * peers)
        add_rows(expo, scale, mass, blocks)

        @pl.when(step == steps - 1)
        def _():
            put_mass(mass, line, blocks)
            out_ref[...] = jnp.broadcast_to(line[...][None], out_ref.shape)

    return call(
        body,
        steps,
        [
            pl.BlockSpec(memory_space=pltpu.SMEM),
            whole(own_half.shape),
            whole(own_half.shape),
            whole(shared.shape),
            pl.BlockSpec((T_CHUNK, width), lambda c: (c, 0)),
        ],
        [
            whole(full),
            whole((blocks * tr, LANES)),
            whole((peers, blocks * tr, LANES)),
        ],
        [
            struct(full, BF16),
            struct((blocks * tr, LANES)),
            struct((peers, blocks * tr, LANES)),
        ],
        [
            pltpu.VMEM((max(blocks, 8), t_rows), F32),
            pltpu.VMEM((blocks, T_CHUNK, t_rows), F32),
            pltpu.VMEM((blocks, 8, t_rows), F32),
            pltpu.VMEM((blocks * tr, LANES), F32),
        ],
        2 * columns * width * t_rows * blocks,
        columns * t_rows * blocks,
        5 * 2**20,
    )(core, own_half, other_half, shared, wt)


def next_iteration(feats, old, received, wt):
    blocks, width, t_rows = feats.shape
    columns = wt.shape[0]
    peers = received.shape[0]
    steps = columns // T_CHUNK
    tr = t_rows // LANES
    total_t = blocks * t_rows

    def body(feat_ref, old_ref, recv_ref, wt_ref, off_out, out_ref, offset, expo, mass, line):
        step = pl.program_id(0)

        @pl.when(step == 0)
        def _():
            packed = old_ref[...] + jnp.log2(total_t * jnp.sum(recv_ref[...], axis=0))
            off_out[...] = packed
            fill_offsets(offset, packed, blocks, tr)
            mass[...] = jnp.zeros_like(mass)

        scale = expos_and_scale(wt_ref[...], feat_ref, offset, expo, blocks, columns * peers)
        add_rows(expo, scale, mass, blocks)

        @pl.when(step == steps - 1)
        def _():
            put_mass(mass, line, blocks)
            out_ref[...] = jnp.broadcast_to(line[...][None], out_ref.shape)

    return call(
        body,
        steps,
        [
            whole(feats.shape),
            whole(old.shape),
            whole(received.shape),
            pl.BlockSpec((T_CHUNK, width), lambda c: (c, 0)),
        ],
        [whole(old.shape), whole((peers, blocks * tr, LANES))],
        [struct(old.shape), struct((peers, blocks * tr, LANES))],
        [
            pltpu.VMEM((max(blocks, 8), t_rows), F32),
            pltpu.VMEM((blocks, T_CHUNK, t_rows), F32),
            pltpu.VMEM((blocks, 8, t_rows), F32),
            pltpu.VMEM((blocks * tr, LANES), F32),
        ],
        2 * columns * width * t_rows * blocks,
        columns * t_rows * blocks,
        4 * 2**20,
    )(feats, old, received, wt)


def last_iteration(me, feats, old, received, w, wt, gt):
    blocks, width, t_rows = feats.shape
    columns = wt.shape[0]
    peers = received.shape[0]
    steps = columns // T_CHUNK
    tr = t_rows // LANES
    total_t = blocks * t_rows
    lines = -(-(blocks * tr + tr) // 8) * 8

    def body(
        me_ref, feat_ref, old_ref, recv_ref, w_ref, wt_ref, gt_ref,
        off_out, scale_out, taught_ref, out_ref, offset, expo, mass, line, acc,
    ):
        step = pl.program_id(0)

        @pl.when(step == 0)
        def _():
            packed = old_ref[...] + jnp.log2(total_t * jnp.sum(recv_ref[...], axis=0))
            off_out[...] = packed
            fill_offsets(offset, packed, blocks, tr)
            mass[...] = jnp.zeros_like(mass)
            acc[...] = jnp.zeros_like(acc)

        scale = expos_and_scale(wt_ref[...], feat_ref, offset, expo, blocks, columns * peers)
        scale_out[...] = jnp.broadcast_to(scale, scale_out.shape)
        add_rows(expo, scale, mass, blocks)
        high, low = halves(expo[me_ref[0]] * scale)
        acc[...] += mm(w_ref[...], high, NN) + mm(w_ref[...], low, NN)

        @pl.when(step == steps - 1)
        def _():
            line[...] = jnp.zeros_like(line)
            put_mass(mass, line, blocks)
            put_rows(line, blocks * tr, jnp.sum(acc[...] * gt_ref[...], axis=0, keepdims=True))
            out_ref[...] = jnp.broadcast_to(line[...][None], out_ref.shape)
            taught_ref[...] = acc[...]

    return call(
        body,
        steps,
        [
            pl.BlockSpec(memory_space=pltpu.SMEM),
            whole(feats.shape),
            whole(old.shape),
            whole(received.shape),
            pl.BlockSpec((width, T_CHUNK), lambda c: (0, c)),
            pl.BlockSpec((T_CHUNK, width), lambda c: (c, 0)),
            whole(gt.shape),
        ],
        [
            whole(old.shape),
            pl.BlockSpec((T_CHUNK, LANES), lambda c: (c, 0)),
            whole((width, t_rows)),
            whole((peers, lines, LANES)),
        ],
        [
            struct(old.shape),
            struct((columns, LANES)),
            struct((width, t_rows)),
            struct((peers, lines, LANES)),
        ],
        [
            pltpu.VMEM((max(blocks, 8), t_rows), F32),
            pltpu.VMEM((blocks, T_CHUNK, t_rows), F32),
            pltpu.VMEM((blocks, 8, t_rows), F32),
            pltpu.VMEM((lines, LANES), F32),
            pltpu.VMEM((width, t_rows), F32),
        ],
        2 * columns * width * t_rows * (blocks + 2),
        columns * t_rows * blocks,
        8 * 2**20,
    )(me, feats, old, received, w, wt, gt)


def after_iterations(me, received, lse, taught, onehot, ds_prob, blocks):
    width, t_rows = taught.shape
    tr = t_rows // LANES
    n = blocks * tr

    def body(me_ref, recv_ref, lse_ref, taught_ref, oh_ref, prob_ref, part_ref, log_ref, ds_ref):
        total = jnp.sum(recv_ref[...], axis=0)
        log_ref[...] = jnp.log2(total[:n])
        start = me_ref[0] * tr
        inverse = 1.0 / jnp.sum(recv_ref[:, pl.ds(start, tr), :], axis=0)
        product = jnp.sum(total[n : n + tr] * inverse) / STUDENT_TEMP
        part_ref[...] = jnp.full(part_ref.shape, jnp.sum(lse_ref[...]) / LOG2E - product, F32)
        row = jnp.concatenate([inverse[i : i + 1, :] for i in range(tr)], axis=1)
        high, low = halves(taught_ref[...] * row / STUDENT_TEMP)
        wanted = mm(oh_ref[...], high, NT) + mm(oh_ref[...], low, NT)
        ds_ref[...] = prob_ref[...] - wanted.reshape(ds_ref.shape)

    return call(
        body,
        1,
        [
            pl.BlockSpec(memory_space=pltpu.SMEM),
            whole(received.shape),
            whole(lse.shape),
            whole(taught.shape),
            whole(onehot.shape),
            whole(ds_prob.shape),
        ],
        [whole((blocks, 8, LANES)), whole((n, LANES)), whole(ds_prob.shape)],
        [struct((blocks, 8, LANES)), struct((n, LANES)), struct(ds_prob.shape)],
        [],
        4 * onehot.size * width,
        1024,
        3 * 2**20,
    )(me, received, lse, taught, onehot, ds_prob)


def weight_grad(feats, old, log_mass, wt, shared, scale, prob_part):
    blocks, width, t_rows = feats.shape
    columns = wt.shape[0]
    steps = columns // T_CHUNK
    tr = t_rows // LANES
    share = shared.shape[1] - 8

    def body(feat_ref, old_ref, log_ref, wt_ref, sh_ref, scale_ref, prob_ref, out_ref, offset, g):
        step = pl.program_id(0)

        @pl.when(step == 0)
        def _():
            fill_offsets(offset, old_ref[...] + log_ref[...], blocks, tr)
            for i in range(blocks):
                high, low = halves(sh_ref[i, :share, :])
                g[i] = jnp.concatenate([high, low, jnp.zeros((LANES - 2 * share, t_rows), BF16)])

        acc = jnp.zeros((T_CHUNK, LANES), F32)
        for i in range(blocks):
            scores = mm(wt_ref[...], feat_ref[i], NN)
            high, low = halves(jnp.exp2(scores * T_SCALE - offset[i : i + 1, :]))
            acc += mm(high, g[i], NT) + mm(low, g[i], NT)
        turned = (acc * scale_ref[...]).T
        taught = turned[:share] + turned[share : 2 * share]
        out_ref[...] = prob_ref[...] - taught / STUDENT_TEMP

    return call(
        body,
        steps,
        [
            whole(feats.shape),
            whole(old.shape),
            whole(log_mass.shape),
            pl.BlockSpec((T_CHUNK, width), lambda c: (c, 0)),
            whole(shared.shape),
            pl.BlockSpec((T_CHUNK, LANES), lambda c: (c, 0)),
            pl.BlockSpec((share, T_CHUNK), lambda c: (0, c)),
        ],
        [pl.BlockSpec((share, T_CHUNK), lambda c: (0, c))],
        [struct((share, columns))],
        [
            pltpu.VMEM((max(blocks, 8), t_rows), F32),
            pltpu.VMEM((blocks, LANES, t_rows), BF16),
        ],
        2 * columns * width * t_rows * blocks * 3,
        columns * t_rows * blocks,
        6 * 2**20,
    )(feats, old, log_mass, wt, shared, scale, prob_part)[0]


def per_device(tf, sf, w, pairing):
    t_rows = tf.shape[0]
    rows = sf.shape[0]
    blocks = lax.axis_size("batch")
    peers = lax.axis_size("proto")
    me = lax.axis_index("batch").astype(jnp.int32).reshape(1)
    core = lax.rem(lax.axis_index("proto"), 2).astype(jnp.int32)

    def swap(x, axis):
        return lax.all_to_all(x, axis, 0, 0)

    core = core.reshape(1)
    own_half = lax.all_gather(core_half(core, tf), "batch")
    other_half = lax.ppermute(own_half, "proto", [(i, i ^ 1) for i in range(peers)])
    pairs = pairing - me * t_rows
    onehot = (pairs[:, None] == jnp.arange(t_rows, dtype=jnp.int32)[None, :]).astype(BF16)
    wt, gt, stats = student_stats(sf, tf, w, onehot, peers)
    stats = swap(stats, "proto")
    lse, shared = merge_stats(stats, gt, rows, blocks)
    shared = swap(shared, "batch")
    before = student_grads(sf, w, wt, lse, 0, None, peers)

    feats, offset, mass = first_iteration(
        core, own_half, other_half, shared, wt, peers
    )
    lse_late, offset = lax.optimization_barrier((lse, offset))
    ds_prob, dw_prob = student_grads(sf, w, wt, lse_late, 1, before, peers)
    dw_prob = lax.psum_scatter(dw_prob, "batch", scatter_dimension=0, tiled=True)
    for _ in range(ITERS - 2):
        offset, mass = next_iteration(feats, offset, swap(mass, "proto"), wt)
    offset, scale, taught, mass = last_iteration(
        me, feats, offset, swap(mass, "proto"), w, wt, gt
    )
    mass = swap(mass, "proto")
    loss, log_mass, ds = after_iterations(me, mass, lse, taught, onehot, ds_prob, blocks)
    ds = swap(ds, "proto")
    loss = swap(loss, "batch")
    d_weight = weight_grad(feats, offset, log_mass, wt, shared, scale, dw_prob)
    d_student = jnp.sum(ds, axis=0)
    loss = jnp.sum(loss[:, 0, 0]) / (rows * blocks)
    return loss, d_student, d_weight


def solution(mesh):
    placed = (P("batch", None), P("batch", None), P(None, "proto"), P("batch"))
    return jax.shard_map(
        per_device,
        mesh=mesh,
        in_specs=placed,
        out_specs=(P(), P(("batch", "proto"), None), P("batch", "proto")),
        check_vma=False,
    )
```

```python
import math

import jax
import jax.numpy as jnp
from jax import lax
from jax.experimental import pallas as pl
from jax.experimental.pallas import tpu as pltpu
from jax.sharding import PartitionSpec as P

ITERS = 3
LANES = 128
S_CHUNK = 512
T_CHUNK = 512
TEACHER_TEMP = 0.07
STUDENT_TEMP = 0.1
LOG2E = math.log2(math.e)
T_SCALE = LOG2E / TEACHER_TEMP
S_SCALE = LOG2E / STUDENT_TEMP
F32 = jnp.float32
BF16 = jnp.bfloat16
NN = (((1,), (0,)), ((), ()))
NT = (((1,), (1,)), ((), ()))
TN = (((0,), (0,)), ((), ()))
VMEM_LIMIT = 40 * 1024 * 1024


def mm(a, b, dims):
    return lax.dot_general(a, b, dims, preferred_element_type=F32)


def halves(x):
    high = x.astype(BF16)
    return high, (x - high.astype(F32)).astype(BF16)


def by_sublane(x, combine):
    return combine(x.reshape(x.shape[0] // 8, 8, x.shape[1]), axis=0)


def whole(shape):
    return pl.BlockSpec(shape, lambda c: (0,) * len(shape))


def call(
    body, grid, in_specs, out_specs, out_shape, scratch, flops, transcendentals, size, aliases=None
):
    return pl.pallas_call(
        body,
        grid=(grid,),
        in_specs=in_specs,
        out_specs=out_specs,
        out_shape=out_shape,
        scratch_shapes=scratch,
        input_output_aliases=aliases or {},
        cost_estimate=pl.CostEstimate(
            flops=flops, transcendentals=transcendentals, bytes_accessed=size
        ),
        compiler_params=pltpu.CompilerParams(
            dimension_semantics=("arbitrary",), vmem_limit_bytes=VMEM_LIMIT
        ),
    )


def struct(shape, dtype=F32):
    return jax.ShapeDtypeStruct(shape, dtype)


def put_rows(ref, first, row):
    for i in range(row.shape[1] // LANES):
        ref[first + i : first + i + 1, :] = row[:, i * LANES : (i + 1) * LANES]


def turned(tf):
    def body(tf_ref, out_ref):
        out_ref[...] = tf_ref[...].astype(F32).T

    return call(
        body, 1, [whole(tf.shape)], [whole(tf.shape[::-1])], [struct(tf.shape[::-1])], [], 0, 0, 2**18
    )(tf)[0]


def student_stats(sf, tf, w, onehot, peers):
    rows, width = sf.shape
    t_rows = tf.shape[0]
    columns = w.shape[1]
    steps = columns // S_CHUNK
    s_rows, tr = rows // LANES, t_rows // LANES
    lines = -(-(2 * s_rows + tr) // 8) * 8

    def body(sf_ref, tf_ref, w_ref, oh_ref, wt_ref, gt_ref, out_ref, high, total, t_high, line):
        step = pl.program_id(0)

        @pl.when(step == 0)
        def _():
            high[...] = jnp.full_like(high, -3e38)
            total[...] = jnp.zeros_like(total)
            t_high[...] = jnp.full_like(t_high, -3e38)
            gt_ref[...] = mm(sf_ref[...], oh_ref[...], TN)

        wt = w_ref[...].T
        wt_ref[...] = wt
        scores = mm(wt, sf_ref[...], NT)
        before = high[...]
        now = jnp.maximum(before, by_sublane(scores, jnp.max))
        high[...] = now
        groups = scores.reshape(S_CHUNK // 8, 8, rows)
        part = jnp.sum(jnp.exp2((groups - now[None]) * S_SCALE), axis=0)
        total[...] = total[...] * jnp.exp2((before - now) * S_SCALE) + part
        t_high[...] = jnp.maximum(t_high[...], by_sublane(mm(wt, tf_ref[...], NT), jnp.max))

        @pl.when(step == steps - 1)
        def _():
            best = jnp.max(high[...], axis=0, keepdims=True)
            summed = jnp.sum(
                total[...] * jnp.exp2((high[...] - best) * S_SCALE), axis=0, keepdims=True
            )
            line[...] = jnp.zeros_like(line)
            put_rows(line, 0, best)
            put_rows(line, s_rows, summed)
            put_rows(line, 2 * s_rows, jnp.max(t_high[...], axis=0, keepdims=True))
            out_ref[...] = jnp.broadcast_to(line[...][None], out_ref.shape)

    return call(
        body,
        steps,
        [
            whole(sf.shape),
            whole(tf.shape),
            pl.BlockSpec((width, S_CHUNK), lambda c: (0, c)),
            whole(onehot.shape),
        ],
        [
            pl.BlockSpec((S_CHUNK, width), lambda c: (c, 0)),
            whole((width, t_rows)),
            whole((peers, lines, LANES)),
        ],
        [
            struct((columns, width), BF16),
            struct((width, t_rows)),
            struct((peers, lines, LANES)),
        ],
        [
            pltpu.VMEM((8, rows), F32),
            pltpu.VMEM((8, rows), F32),
            pltpu.VMEM((8, t_rows), F32),
            pltpu.VMEM((lines, LANES), F32),
        ],
        2 * columns * width * (rows + t_rows),
        columns * rows,
        8 * 2**20,
    )(sf, tf, w, onehot)


def merge_stats(stats, gt, rows, batches):
    width, t_rows = gt.shape
    share = width // batches
    s_rows, tr = rows // LANES, t_rows // LANES

    def body(stats_ref, gt_ref, lse_ref, out_ref):
        highs = stats_ref[:, :s_rows, :]
        best = jnp.max(highs, axis=0)
        total = jnp.sum(
            stats_ref[:, s_rows : 2 * s_rows, :] * jnp.exp2((highs - best[None]) * S_SCALE), axis=0
        )
        lse_ref[...] = best * S_SCALE + jnp.log2(total)
        t_best = jnp.max(stats_ref[:, 2 * s_rows : 2 * s_rows + tr, :], axis=0) * T_SCALE
        row = jnp.concatenate([t_best[i : i + 1, :] for i in range(tr)], axis=1)
        for b in range(batches):
            out_ref[b, :share, :] = gt_ref[b * share : (b + 1) * share, :]
            out_ref[b, share:, :] = jnp.broadcast_to(row, (8, t_rows))

    return call(
        body,
        1,
        [whole(stats.shape), whole(gt.shape)],
        [whole((s_rows, LANES)), whole((batches, share + 8, t_rows))],
        [struct((s_rows, LANES)), struct((batches, share + 8, t_rows))],
        [],
        stats.size * 4,
        stats.size,
        2**21,
    )(stats, gt)


def student_grads(sf, w, wt, lse, peers):
    rows, width = sf.shape
    columns = w.shape[1]
    steps = columns // S_CHUNK
    s_rows = rows // LANES

    def body(sf_ref, w_ref, wt_ref, lse_ref, ds_ref, dw_ref, lse_row, sft, acc):
        step = pl.program_id(0)

        @pl.when(step == 0)
        def _():
            for i in range(s_rows):
                lse_row[:, i * LANES : (i + 1) * LANES] = lse_ref[i : i + 1, :]
            sft[...] = sf_ref[...].T
            acc[...] = jnp.zeros_like(acc)

        scores = mm(wt_ref[...], sf_ref[...], NT)
        high, low = halves(jnp.exp2(scores * S_SCALE - lse_row[...]))
        acc[...] += mm(w_ref[...], high, NN) + mm(w_ref[...], low, NN)
        dw_ref[...] = (mm(sft[...], high, NT) + mm(sft[...], low, NT)) / STUDENT_TEMP

        @pl.when(step == steps - 1)
        def _():
            ds_ref[...] = (acc[...].T / STUDENT_TEMP).reshape(ds_ref.shape)

    return call(
        body,
        steps,
        [
            whole(sf.shape),
            pl.BlockSpec((width, S_CHUNK), lambda c: (0, c)),
            pl.BlockSpec((S_CHUNK, width), lambda c: (c, 0)),
            whole(lse.shape),
        ],
        [
            whole((peers, rows // peers, width)),
            pl.BlockSpec((width, S_CHUNK), lambda c: (0, c)),
        ],
        [struct((peers, rows // peers, width)), struct((width, columns))],
        [
            pltpu.VMEM((1, rows), F32),
            pltpu.VMEM((width, rows), BF16),
            pltpu.VMEM((width, rows), F32),
        ],
        16 * columns * width * rows,
        columns * rows,
        10 * 2**20,
    )(sf, w, wt, lse)


def fill_offsets(offset, packed, blocks, per_block):
    for i in range(blocks):
        for j in range(per_block):
            line = i * per_block + j
            offset[i : i + 1, j * LANES : (j + 1) * LANES] = packed[line : line + 1, :]


def expos_and_scale(wt, feats, offset, expo, blocks, all_columns):
    partial = None
    for i in range(blocks):
        scores = mm(wt, feats[i], NN)
        values = jnp.exp2(scores * T_SCALE - offset[i : i + 1, :])
        expo[i] = values
        for j in range(values.shape[1] // LANES):
            piece = values[:, j * LANES : (j + 1) * LANES]
            partial = piece if partial is None else partial + piece
    return 1.0 / (all_columns * jnp.sum(partial, axis=1, keepdims=True))


def add_rows(expo, scale, mass, blocks):
    for i in range(blocks):
        mass[i] += by_sublane(expo[i] * scale, jnp.sum)


def put_mass(mass, line, blocks):
    for i in range(blocks):
        row = jnp.sum(mass[i], axis=0, keepdims=True)
        put_rows(line, i * (row.shape[1] // LANES), row)


def first_iteration(feats_f32, shared, wt, passed, peers):
    blocks, width, t_rows = feats_f32.shape
    columns = wt.shape[0]
    steps = columns // T_CHUNK
    tr = t_rows // LANES
    share = shared.shape[1] - 8

    def body(
        feat_ref, shared_ref, wt_ref, _,
        feat_out, off_out, out_ref, __, offset, expo, mass, line,
    ):
        step = pl.program_id(0)

        @pl.when(step == 0)
        def _():
            feat_out[...] = feat_ref[...].astype(BF16)
            for i in range(blocks):
                row = shared_ref[i, share : share + 1, :]
                offset[i : i + 1, :] = row
                put_rows(off_out, i * tr, row)
            mass[...] = jnp.zeros_like(mass)

        scale = expos_and_scale(wt_ref[...], feat_out, offset, expo, blocks, columns * peers)
        add_rows(expo, scale, mass, blocks)

        @pl.when(step == steps - 1)
        def _():
            put_mass(mass, line, blocks)
            out_ref[...] = jnp.broadcast_to(line[...][None], out_ref.shape)

    return call(
        body,
        steps,
        [
            whole(feats_f32.shape),
            whole(shared.shape),
            pl.BlockSpec((T_CHUNK, width), lambda c: (c, 0)),
            pl.BlockSpec(memory_space=pl.ANY),
        ],
        [
            whole(feats_f32.shape),
            whole((blocks * tr, LANES)),
            whole((peers, blocks * tr, LANES)),
            pl.BlockSpec(memory_space=pl.ANY),
        ],
        [
            struct(feats_f32.shape, BF16),
            struct((blocks * tr, LANES)),
            struct((peers, blocks * tr, LANES)),
            struct(passed.shape),
        ],
        [
            pltpu.VMEM((max(blocks, 8), t_rows), F32),
            pltpu.VMEM((blocks, T_CHUNK, t_rows), F32),
            pltpu.VMEM((blocks, 8, t_rows), F32),
            pltpu.VMEM((blocks * tr, LANES), F32),
        ],
        5 * columns * width * t_rows * blocks,
        columns * t_rows * blocks,
        5 * 2**20,
        {3: 3},
    )(feats_f32, shared, wt, passed)


def next_iteration(feats, old, received, wt):
    blocks, width, t_rows = feats.shape
    columns = wt.shape[0]
    peers = received.shape[0]
    steps = columns // T_CHUNK
    tr = t_rows // LANES
    total_t = blocks * t_rows

    def body(feat_ref, old_ref, recv_ref, wt_ref, off_out, out_ref, offset, expo, mass, line):
        step = pl.program_id(0)

        @pl.when(step == 0)
        def _():
            packed = old_ref[...] + jnp.log2(total_t * jnp.sum(recv_ref[...], axis=0))
            off_out[...] = packed
            fill_offsets(offset, packed, blocks, tr)
            mass[...] = jnp.zeros_like(mass)

        scale = expos_and_scale(wt_ref[...], feat_ref, offset, expo, blocks, columns * peers)
        add_rows(expo, scale, mass, blocks)

        @pl.when(step == steps - 1)
        def _():
            put_mass(mass, line, blocks)
            out_ref[...] = jnp.broadcast_to(line[...][None], out_ref.shape)

    return call(
        body,
        steps,
        [
            whole(feats.shape),
            whole(old.shape),
            whole(received.shape),
            pl.BlockSpec((T_CHUNK, width), lambda c: (c, 0)),
        ],
        [whole(old.shape), whole((peers, blocks * tr, LANES))],
        [struct(old.shape), struct((peers, blocks * tr, LANES))],
        [
            pltpu.VMEM((max(blocks, 8), t_rows), F32),
            pltpu.VMEM((blocks, T_CHUNK, t_rows), F32),
            pltpu.VMEM((blocks, 8, t_rows), F32),
            pltpu.VMEM((blocks * tr, LANES), F32),
        ],
        2 * columns * width * t_rows * blocks,
        columns * t_rows * blocks,
        4 * 2**20,
    )(feats, old, received, wt)


def last_iteration(me, feats, old, received, w, wt, gt):
    blocks, width, t_rows = feats.shape
    columns = wt.shape[0]
    peers = received.shape[0]
    steps = columns // T_CHUNK
    tr = t_rows // LANES
    total_t = blocks * t_rows
    lines = -(-(blocks * tr + tr) // 8) * 8

    def body(
        me_ref, feat_ref, old_ref, recv_ref, w_ref, wt_ref, gt_ref,
        off_out, scale_out, taught_ref, out_ref, offset, expo, mass, line, acc,
    ):
        step = pl.program_id(0)

        @pl.when(step == 0)
        def _():
            packed = old_ref[...] + jnp.log2(total_t * jnp.sum(recv_ref[...], axis=0))
            off_out[...] = packed
            fill_offsets(offset, packed, blocks, tr)
            mass[...] = jnp.zeros_like(mass)
            acc[...] = jnp.zeros_like(acc)

        scale = expos_and_scale(wt_ref[...], feat_ref, offset, expo, blocks, columns * peers)
        scale_out[...] = jnp.broadcast_to(scale, scale_out.shape)
        add_rows(expo, scale, mass, blocks)
        high, low = halves(expo[me_ref[0]] * scale)
        acc[...] += mm(w_ref[...], high, NN) + mm(w_ref[...], low, NN)

        @pl.when(step == steps - 1)
        def _():
            line[...] = jnp.zeros_like(line)
            put_mass(mass, line, blocks)
            put_rows(line, blocks * tr, jnp.sum(acc[...] * gt_ref[...], axis=0, keepdims=True))
            out_ref[...] = jnp.broadcast_to(line[...][None], out_ref.shape)
            taught_ref[...] = acc[...]

    return call(
        body,
        steps,
        [
            pl.BlockSpec(memory_space=pltpu.SMEM),
            whole(feats.shape),
            whole(old.shape),
            whole(received.shape),
            pl.BlockSpec((width, T_CHUNK), lambda c: (0, c)),
            pl.BlockSpec((T_CHUNK, width), lambda c: (c, 0)),
            whole(gt.shape),
        ],
        [
            whole(old.shape),
            pl.BlockSpec((T_CHUNK, LANES), lambda c: (c, 0)),
            whole((width, t_rows)),
            whole((peers, lines, LANES)),
        ],
        [
            struct(old.shape),
            struct((columns, LANES)),
            struct((width, t_rows)),
            struct((peers, lines, LANES)),
        ],
        [
            pltpu.VMEM((max(blocks, 8), t_rows), F32),
            pltpu.VMEM((blocks, T_CHUNK, t_rows), F32),
            pltpu.VMEM((blocks, 8, t_rows), F32),
            pltpu.VMEM((lines, LANES), F32),
            pltpu.VMEM((width, t_rows), F32),
        ],
        2 * columns * width * t_rows * (blocks + 2),
        columns * t_rows * blocks,
        8 * 2**20,
    )(me, feats, old, received, w, wt, gt)


def after_iterations(me, received, lse, taught, onehot, ds_prob, blocks):
    width, t_rows = taught.shape
    tr = t_rows // LANES
    n = blocks * tr

    def body(me_ref, recv_ref, lse_ref, taught_ref, oh_ref, prob_ref, part_ref, inv_ref, ds_ref):
        total = jnp.sum(recv_ref[...], axis=0)
        inv_ref[...] = 1.0 / total[:n]
        start = me_ref[0] * tr
        inverse = 1.0 / jnp.sum(recv_ref[:, pl.ds(start, tr), :], axis=0)
        product = jnp.sum(total[n : n + tr] * inverse) / STUDENT_TEMP
        part_ref[...] = jnp.full(part_ref.shape, jnp.sum(lse_ref[...]) / LOG2E - product, F32)
        row = jnp.concatenate([inverse[i : i + 1, :] for i in range(tr)], axis=1)
        high, low = halves(taught_ref[...] * row / STUDENT_TEMP)
        wanted = mm(oh_ref[...], high, NT) + mm(oh_ref[...], low, NT)
        ds_ref[...] = prob_ref[...] - wanted.reshape(ds_ref.shape)

    return call(
        body,
        1,
        [
            pl.BlockSpec(memory_space=pltpu.SMEM),
            whole(received.shape),
            whole(lse.shape),
            whole(taught.shape),
            whole(onehot.shape),
            whole(ds_prob.shape),
        ],
        [whole((blocks, 8, LANES)), whole((n, LANES)), whole(ds_prob.shape)],
        [struct((blocks, 8, LANES)), struct((n, LANES)), struct(ds_prob.shape)],
        [],
        4 * onehot.size * width,
        1024,
        3 * 2**20,
    )(me, received, lse, taught, onehot, ds_prob)


def split_expos(feats, offset_packed, wt):
    blocks, width, t_rows = feats.shape
    columns = wt.shape[0]
    steps = columns // T_CHUNK
    tr = t_rows // LANES
    block = pl.BlockSpec((blocks, T_CHUNK, t_rows), lambda c: (0, c, 0))

    def body(feat_ref, off_ref, wt_ref, high_ref, low_ref, offset):
        @pl.when(pl.program_id(0) == 0)
        def _():
            fill_offsets(offset, off_ref[...], blocks, tr)

        for i in range(blocks):
            scores = mm(wt_ref[...], feat_ref[i], NN)
            high, low = halves(jnp.exp2(scores * T_SCALE - offset[i : i + 1, :]))
            high_ref[i] = high
            low_ref[i] = low

    return call(
        body,
        steps,
        [
            whole(feats.shape),
            whole(offset_packed.shape),
            pl.BlockSpec((T_CHUNK, width), lambda c: (c, 0)),
        ],
        [block, block],
        [struct((blocks, columns, t_rows), BF16)] * 2,
        [pltpu.VMEM((max(blocks, 8), t_rows), F32)],
        5 * columns * width * t_rows * blocks,
        columns * t_rows * blocks,
        35 * 2**20,
    )(feats, offset_packed, wt)


def weight_grad(high, low, inverse, shared, scale):
    blocks, columns, t_rows = high.shape
    steps = columns // T_CHUNK
    tr = t_rows // LANES
    share = shared.shape[1] - 8
    block = pl.BlockSpec((blocks, T_CHUNK, t_rows), lambda c: (0, c, 0))

    def body(high_ref, low_ref, inv_ref, sh_ref, scale_ref, out_ref, factor, g):
        @pl.when(pl.program_id(0) == 0)
        def _():
            fill_offsets(factor, inv_ref[...], blocks, tr)
            for i in range(blocks):
                part = sh_ref[i, :share, :] * factor[i : i + 1, :] / STUDENT_TEMP
                first, second = halves(part)
                g[i] = jnp.concatenate(
                    [first, second, jnp.zeros((LANES - 2 * share, t_rows), BF16)]
                )

        acc = jnp.zeros((T_CHUNK, LANES), F32)
        for i in range(blocks):
            acc += mm(high_ref[i], g[i], NT) + mm(low_ref[i], g[i], NT)
        out = (acc * scale_ref[...]).T
        out_ref[...] = out[:share] + out[share : 2 * share]

    return call(
        body,
        steps,
        [
            block,
            block,
            whole(inverse.shape),
            whole(shared.shape),
            pl.BlockSpec((T_CHUNK, LANES), lambda c: (c, 0)),
        ],
        [pl.BlockSpec((share, T_CHUNK), lambda c: (0, c))],
        [struct((share, columns))],
        [
            pltpu.VMEM((max(blocks, 8), t_rows), F32),
            pltpu.VMEM((blocks, LANES, t_rows), BF16),
        ],
        5 * columns * t_rows * t_rows * blocks,
        0,
        35 * 2**20,
    )(high, low, inverse, shared, scale)[0]


def per_device(tf, sf, w, pairing):
    t_rows = tf.shape[0]
    rows = sf.shape[0]
    blocks = lax.axis_size("batch")
    peers = lax.axis_size("proto")
    me = lax.axis_index("batch").astype(jnp.int32).reshape(1)

    def swap(x, axis):
        return lax.all_to_all(x, axis, 0, 0)

    feats_f32 = lax.all_gather(turned(tf), "batch")
    pairs = pairing - me * t_rows
    onehot = (pairs[:, None] == jnp.arange(t_rows, dtype=jnp.int32)[None, :]).astype(BF16)
    wt, gt, stats = student_stats(sf, tf, w, onehot, peers)
    stats = swap(stats, "proto")
    lse, shared = merge_stats(stats, gt, rows, blocks)
    shared = swap(shared, "batch")
    ds_prob, dw_prob = student_grads(sf, w, wt, lse, peers)

    feats, offset, mass, dw_prob = first_iteration(feats_f32, shared, wt, dw_prob, peers)
    dw_prob = lax.psum_scatter(dw_prob, "batch", scatter_dimension=0, tiled=True)
    for _ in range(ITERS - 2):
        offset, mass = next_iteration(feats, offset, swap(mass, "proto"), wt)
    offset, scale, taught, mass = last_iteration(
        me, feats, offset, swap(mass, "proto"), w, wt, gt
    )
    mass = swap(mass, "proto")
    high, low = split_expos(feats, offset, wt)
    loss, inverse, ds = after_iterations(me, mass, lse, taught, onehot, ds_prob, blocks)
    ds = swap(ds, "proto")
    loss = swap(loss, "batch")
    d_weight = dw_prob - weight_grad(high, low, inverse, shared, scale)
    d_student = jnp.sum(ds, axis=0)
    loss = jnp.sum(loss[:, 0, 0]) / (rows * blocks)
    return loss, d_student, d_weight


def solution(mesh):
    placed = (P("batch", None), P("batch", None), P(None, "proto"), P("batch"))
    return jax.shard_map(
        per_device,
        mesh=mesh,
        in_specs=placed,
        out_specs=(P(), P(("batch", "proto"), None), P("batch", "proto")),
        check_vma=False,
    )
```

```python
import math

import jax
import jax.numpy as jnp
from jax import lax
from jax.experimental import pallas as pl
from jax.experimental.pallas import tpu as pltpu
from jax.sharding import PartitionSpec as P

ITERS = 3
LANES = 128
S_CHUNK = 512
T_CHUNK = 1024
TEACHER_TEMP = 0.07
STUDENT_TEMP = 0.1
LOG2E = math.log2(math.e)
T_SCALE = LOG2E / TEACHER_TEMP
S_SCALE = LOG2E / STUDENT_TEMP
F32 = jnp.float32
BF16 = jnp.bfloat16
NN = (((1,), (0,)), ((), ()))
NT = (((1,), (1,)), ((), ()))
TN = (((0,), (0,)), ((), ()))
VMEM_LIMIT = 60 * 1024 * 1024


def mm(a, b, dims):
    return lax.dot_general(a, b, dims, preferred_element_type=F32)


def halves(x):
    high = x.astype(BF16)
    return high, (x - high.astype(F32)).astype(BF16)


def by_sublane(x, combine):
    return combine(x.reshape(x.shape[0] // 8, 8, x.shape[1]), axis=0)


def whole(shape):
    return pl.BlockSpec(shape, lambda c: (0,) * len(shape))


def call(
    body, grid, in_specs, out_specs, out_shape, scratch, flops, transcendentals, size, aliases=None
):
    return pl.pallas_call(
        body,
        grid=(grid,),
        in_specs=in_specs,
        out_specs=out_specs,
        out_shape=out_shape,
        scratch_shapes=scratch,
        input_output_aliases=aliases or {},
        cost_estimate=pl.CostEstimate(
            flops=flops, transcendentals=transcendentals, bytes_accessed=size
        ),
        compiler_params=pltpu.CompilerParams(
            dimension_semantics=("arbitrary",), vmem_limit_bytes=VMEM_LIMIT
        ),
    )


def struct(shape, dtype=F32):
    return jax.ShapeDtypeStruct(shape, dtype)


def put_rows(ref, first, row):
    for i in range(row.shape[1] // LANES):
        ref[first + i : first + i + 1, :] = row[:, i * LANES : (i + 1) * LANES]


def turned(tf):
    def body(tf_ref, out_ref):
        out_ref[...] = tf_ref[...].astype(F32).T

    return call(
        body, 1, [whole(tf.shape)], [whole(tf.shape[::-1])], [struct(tf.shape[::-1])], [], 0, 0, 2**18
    )(tf)[0]


def student_stats(sf, tf, w, onehot, peers):
    rows, width = sf.shape
    t_rows = tf.shape[0]
    columns = w.shape[1]
    steps = columns // S_CHUNK
    s_rows, tr = rows // LANES, t_rows // LANES
    lines = -(-(2 * s_rows + tr) // 8) * 8

    def body(sf_ref, tf_ref, w_ref, oh_ref, wt_ref, gt_ref, out_ref, high, total, t_high, line):
        step = pl.program_id(0)

        @pl.when(step == 0)
        def _():
            high[...] = jnp.full_like(high, -3e38)
            total[...] = jnp.zeros_like(total)
            t_high[...] = jnp.full_like(t_high, -3e38)
            gt_ref[...] = mm(sf_ref[...], oh_ref[...], TN)

        wt = w_ref[...].T
        wt_ref[...] = wt
        scores = mm(wt, sf_ref[...], NT)
        before = high[...]
        now = jnp.maximum(before, by_sublane(scores, jnp.max))
        high[...] = now
        groups = scores.reshape(S_CHUNK // 8, 8, rows)
        part = jnp.sum(jnp.exp2((groups - now[None]) * S_SCALE), axis=0)
        total[...] = total[...] * jnp.exp2((before - now) * S_SCALE) + part
        t_high[...] = jnp.maximum(t_high[...], by_sublane(mm(wt, tf_ref[...], NT), jnp.max))

        @pl.when(step == steps - 1)
        def _():
            best = jnp.max(high[...], axis=0, keepdims=True)
            summed = jnp.sum(
                total[...] * jnp.exp2((high[...] - best) * S_SCALE), axis=0, keepdims=True
            )
            line[...] = jnp.zeros_like(line)
            put_rows(line, 0, best)
            put_rows(line, s_rows, summed)
            put_rows(line, 2 * s_rows, jnp.max(t_high[...], axis=0, keepdims=True))
            out_ref[...] = jnp.broadcast_to(line[...][None], out_ref.shape)

    return call(
        body,
        steps,
        [
            whole(sf.shape),
            whole(tf.shape),
            pl.BlockSpec((width, S_CHUNK), lambda c: (0, c)),
            whole(onehot.shape),
        ],
        [
            pl.BlockSpec((S_CHUNK, width), lambda c: (c, 0)),
            whole((width, t_rows)),
            whole((peers, lines, LANES)),
        ],
        [
            struct((columns, width), BF16),
            struct((width, t_rows)),
            struct((peers, lines, LANES)),
        ],
        [
            pltpu.VMEM((8, rows), F32),
            pltpu.VMEM((8, rows), F32),
            pltpu.VMEM((8, t_rows), F32),
            pltpu.VMEM((lines, LANES), F32),
        ],
        2 * columns * width * (rows + t_rows),
        columns * rows,
        8 * 2**20,
    )(sf, tf, w, onehot)


def merge_stats(stats, gt, rows, batches):
    width, t_rows = gt.shape
    share = width // batches
    s_rows, tr = rows // LANES, t_rows // LANES

    def body(stats_ref, gt_ref, lse_ref, out_ref):
        highs = stats_ref[:, :s_rows, :]
        best = jnp.max(highs, axis=0)
        total = jnp.sum(
            stats_ref[:, s_rows : 2 * s_rows, :] * jnp.exp2((highs - best[None]) * S_SCALE), axis=0
        )
        lse_ref[...] = best * S_SCALE + jnp.log2(total)
        t_best = jnp.max(stats_ref[:, 2 * s_rows : 2 * s_rows + tr, :], axis=0) * T_SCALE
        row = jnp.concatenate([t_best[i : i + 1, :] for i in range(tr)], axis=1)
        for b in range(batches):
            out_ref[b, :share, :] = gt_ref[b * share : (b + 1) * share, :]
            out_ref[b, share:, :] = jnp.broadcast_to(row, (8, t_rows))

    return call(
        body,
        1,
        [whole(stats.shape), whole(gt.shape)],
        [whole((s_rows, LANES)), whole((batches, share + 8, t_rows))],
        [struct((s_rows, LANES)), struct((batches, share + 8, t_rows))],
        [],
        stats.size * 4,
        stats.size,
        2**21,
    )(stats, gt)


def student_grads(sf, w, wt, lse, peers):
    rows, width = sf.shape
    columns = w.shape[1]
    steps = columns // S_CHUNK
    s_rows = rows // LANES

    def body(sf_ref, w_ref, wt_ref, lse_ref, ds_ref, dw_ref, lse_row, sft, acc):
        step = pl.program_id(0)

        @pl.when(step == 0)
        def _():
            for i in range(s_rows):
                lse_row[:, i * LANES : (i + 1) * LANES] = lse_ref[i : i + 1, :]
            sft[...] = sf_ref[...].T
            acc[...] = jnp.zeros_like(acc)

        scores = mm(wt_ref[...], sf_ref[...], NT)
        high, low = halves(jnp.exp2(scores * S_SCALE - lse_row[...]))
        acc[...] += mm(w_ref[...], high, NN) + mm(w_ref[...], low, NN)
        dw_ref[...] = (mm(sft[...], high, NT) + mm(sft[...], low, NT)) / STUDENT_TEMP

        @pl.when(step == steps - 1)
        def _():
            ds_ref[...] = (acc[...].T / STUDENT_TEMP).reshape(ds_ref.shape)

    return call(
        body,
        steps,
        [
            whole(sf.shape),
            pl.BlockSpec((width, S_CHUNK), lambda c: (0, c)),
            pl.BlockSpec((S_CHUNK, width), lambda c: (c, 0)),
            whole(lse.shape),
        ],
        [
            whole((peers, rows // peers, width)),
            pl.BlockSpec((width, S_CHUNK), lambda c: (0, c)),
        ],
        [struct((peers, rows // peers, width)), struct((width, columns))],
        [
            pltpu.VMEM((1, rows), F32),
            pltpu.VMEM((width, rows), BF16),
            pltpu.VMEM((width, rows), F32),
        ],
        16 * columns * width * rows,
        columns * rows,
        10 * 2**20,
    )(sf, w, wt, lse)


def fill_offsets(offset, packed, blocks, per_block):
    for i in range(blocks):
        for j in range(per_block):
            line = i * per_block + j
            offset[i : i + 1, j * LANES : (j + 1) * LANES] = packed[line : line + 1, :]


def expos_and_scale(wt, feats, offset, expo, blocks, all_columns):
    partial = None
    for i in range(blocks):
        scores = mm(wt, feats[i], NN)
        values = jnp.exp2(scores * T_SCALE - offset[i : i + 1, :])
        expo[i] = values
        for j in range(values.shape[1] // LANES):
            piece = values[:, j * LANES : (j + 1) * LANES]
            partial = piece if partial is None else partial + piece
    return 1.0 / (all_columns * jnp.sum(partial, axis=1, keepdims=True))


def add_rows(expo, scale, mass, blocks):
    for i in range(blocks):
        mass[i] += by_sublane(expo[i] * scale, jnp.sum)


def put_mass(mass, line, blocks):
    for i in range(blocks):
        row = jnp.sum(mass[i], axis=0, keepdims=True)
        put_rows(line, i * (row.shape[1] // LANES), row)


def first_iteration(feats_f32, shared, wt, passed, peers):
    blocks, width, t_rows = feats_f32.shape
    columns = wt.shape[0]
    steps = columns // T_CHUNK
    tr = t_rows // LANES
    share = shared.shape[1] - 8

    def body(
        feat_ref, shared_ref, wt_ref, _,
        feat_out, off_out, out_ref, __, offset, expo, mass, line,
    ):
        step = pl.program_id(0)

        @pl.when(step == 0)
        def _():
            feat_out[...] = feat_ref[...].astype(BF16)
            for i in range(blocks):
                row = shared_ref[i, share : share + 1, :]
                offset[i : i + 1, :] = row
                put_rows(off_out, i * tr, row)
            mass[...] = jnp.zeros_like(mass)

        scale = expos_and_scale(wt_ref[...], feat_out, offset, expo, blocks, columns * peers)
        add_rows(expo, scale, mass, blocks)

        @pl.when(step == steps - 1)
        def _():
            put_mass(mass, line, blocks)
            out_ref[...] = jnp.broadcast_to(line[...][None], out_ref.shape)

    return call(
        body,
        steps,
        [
            whole(feats_f32.shape),
            whole(shared.shape),
            pl.BlockSpec((T_CHUNK, width), lambda c: (c, 0)),
            pl.BlockSpec(memory_space=pl.ANY),
        ],
        [
            whole(feats_f32.shape),
            whole((blocks * tr, LANES)),
            whole((peers, blocks * tr, LANES)),
            pl.BlockSpec(memory_space=pl.ANY),
        ],
        [
            struct(feats_f32.shape, BF16),
            struct((blocks * tr, LANES)),
            struct((peers, blocks * tr, LANES)),
            struct(passed.shape),
        ],
        [
            pltpu.VMEM((max(blocks, 8), t_rows), F32),
            pltpu.VMEM((blocks, T_CHUNK, t_rows), F32),
            pltpu.VMEM((blocks, 8, t_rows), F32),
            pltpu.VMEM((blocks * tr, LANES), F32),
        ],
        5 * columns * width * t_rows * blocks,
        columns * t_rows * blocks,
        5 * 2**20,
        {3: 3},
    )(feats_f32, shared, wt, passed)


def next_iteration(feats, old, received, wt):
    blocks, width, t_rows = feats.shape
    columns = wt.shape[0]
    peers = received.shape[0]
    steps = columns // T_CHUNK
    tr = t_rows // LANES
    total_t = blocks * t_rows

    def body(feat_ref, old_ref, recv_ref, wt_ref, off_out, out_ref, offset, expo, mass, line):
        step = pl.program_id(0)

        @pl.when(step == 0)
        def _():
            packed = old_ref[...] + jnp.log2(total_t * jnp.sum(recv_ref[...], axis=0))
            off_out[...] = packed
            fill_offsets(offset, packed, blocks, tr)
            mass[...] = jnp.zeros_like(mass)

        scale = expos_and_scale(wt_ref[...], feat_ref, offset, expo, blocks, columns * peers)
        add_rows(expo, scale, mass, blocks)

        @pl.when(step == steps - 1)
        def _():
            put_mass(mass, line, blocks)
            out_ref[...] = jnp.broadcast_to(line[...][None], out_ref.shape)

    return call(
        body,
        steps,
        [
            whole(feats.shape),
            whole(old.shape),
            whole(received.shape),
            pl.BlockSpec((T_CHUNK, width), lambda c: (c, 0)),
        ],
        [whole(old.shape), whole((peers, blocks * tr, LANES))],
        [struct(old.shape), struct((peers, blocks * tr, LANES))],
        [
            pltpu.VMEM((max(blocks, 8), t_rows), F32),
            pltpu.VMEM((blocks, T_CHUNK, t_rows), F32),
            pltpu.VMEM((blocks, 8, t_rows), F32),
            pltpu.VMEM((blocks * tr, LANES), F32),
        ],
        2 * columns * width * t_rows * blocks,
        columns * t_rows * blocks,
        4 * 2**20,
    )(feats, old, received, wt)


def last_iteration(me, feats, old, received, w, wt, gt):
    blocks, width, t_rows = feats.shape
    columns = wt.shape[0]
    peers = received.shape[0]
    steps = columns // T_CHUNK
    tr = t_rows // LANES
    total_t = blocks * t_rows
    lines = -(-(blocks * tr + tr) // 8) * 8

    def body(
        me_ref, feat_ref, old_ref, recv_ref, w_ref, wt_ref, gt_ref,
        off_out, scale_out, taught_ref, out_ref, offset, expo, mass, line, acc,
    ):
        step = pl.program_id(0)

        @pl.when(step == 0)
        def _():
            packed = old_ref[...] + jnp.log2(total_t * jnp.sum(recv_ref[...], axis=0))
            off_out[...] = packed
            fill_offsets(offset, packed, blocks, tr)
            mass[...] = jnp.zeros_like(mass)
            acc[...] = jnp.zeros_like(acc)

        scale = expos_and_scale(wt_ref[...], feat_ref, offset, expo, blocks, columns * peers)
        scale_out[...] = jnp.broadcast_to(scale, scale_out.shape)
        add_rows(expo, scale, mass, blocks)
        high, low = halves(expo[me_ref[0]] * scale)
        acc[...] += mm(w_ref[...], high, NN) + mm(w_ref[...], low, NN)

        @pl.when(step == steps - 1)
        def _():
            line[...] = jnp.zeros_like(line)
            put_mass(mass, line, blocks)
            put_rows(line, blocks * tr, jnp.sum(acc[...] * gt_ref[...], axis=0, keepdims=True))
            out_ref[...] = jnp.broadcast_to(line[...][None], out_ref.shape)
            taught_ref[...] = acc[...]

    return call(
        body,
        steps,
        [
            pl.BlockSpec(memory_space=pltpu.SMEM),
            whole(feats.shape),
            whole(old.shape),
            whole(received.shape),
            pl.BlockSpec((width, T_CHUNK), lambda c: (0, c)),
            pl.BlockSpec((T_CHUNK, width), lambda c: (c, 0)),
            whole(gt.shape),
        ],
        [
            whole(old.shape),
            pl.BlockSpec((T_CHUNK, LANES), lambda c: (c, 0)),
            whole((width, t_rows)),
            whole((peers, lines, LANES)),
        ],
        [
            struct(old.shape),
            struct((columns, LANES)),
            struct((width, t_rows)),
            struct((peers, lines, LANES)),
        ],
        [
            pltpu.VMEM((max(blocks, 8), t_rows), F32),
            pltpu.VMEM((blocks, T_CHUNK, t_rows), F32),
            pltpu.VMEM((blocks, 8, t_rows), F32),
            pltpu.VMEM((lines, LANES), F32),
            pltpu.VMEM((width, t_rows), F32),
        ],
        2 * columns * width * t_rows * (blocks + 2),
        columns * t_rows * blocks,
        8 * 2**20,
    )(me, feats, old, received, w, wt, gt)


def after_iterations(me, received, lse, taught, onehot, ds_prob, blocks):
    width, t_rows = taught.shape
    tr = t_rows // LANES
    n = blocks * tr

    def body(me_ref, recv_ref, lse_ref, taught_ref, oh_ref, prob_ref, part_ref, inv_ref, ds_ref):
        total = jnp.sum(recv_ref[...], axis=0)
        inv_ref[...] = 1.0 / total[:n]
        start = me_ref[0] * tr
        inverse = 1.0 / jnp.sum(recv_ref[:, pl.ds(start, tr), :], axis=0)
        product = jnp.sum(total[n : n + tr] * inverse) / STUDENT_TEMP
        part_ref[...] = jnp.full(part_ref.shape, jnp.sum(lse_ref[...]) / LOG2E - product, F32)
        row = jnp.concatenate([inverse[i : i + 1, :] for i in range(tr)], axis=1)
        high, low = halves(taught_ref[...] * row / STUDENT_TEMP)
        wanted = mm(oh_ref[...], high, NT) + mm(oh_ref[...], low, NT)
        ds_ref[...] = prob_ref[...] - wanted.reshape(ds_ref.shape)

    return call(
        body,
        1,
        [
            pl.BlockSpec(memory_space=pltpu.SMEM),
            whole(received.shape),
            whole(lse.shape),
            whole(taught.shape),
            whole(onehot.shape),
            whole(ds_prob.shape),
        ],
        [whole((blocks, 8, LANES)), whole((n, LANES)), whole(ds_prob.shape)],
        [struct((blocks, 8, LANES)), struct((n, LANES)), struct(ds_prob.shape)],
        [],
        4 * onehot.size * width,
        1024,
        3 * 2**20,
    )(me, received, lse, taught, onehot, ds_prob)


def weight_grad(feats, offset_packed, inverse, wt, shared, scale, all_columns):
    blocks, width, t_rows = feats.shape
    columns = wt.shape[0]
    steps = columns // T_CHUNK
    tr = t_rows // LANES
    share = shared.shape[1] - 8

    def body(feat_ref, off_ref, inv_ref, wt_ref, sh_ref, scale_ref, out_ref, offset, g, g_sum):
        @pl.when(pl.program_id(0) == 0)
        def _():
            fill_offsets(offset, off_ref[...] - jnp.log2(inv_ref[...]), blocks, tr)
            total = jnp.zeros((8, LANES), F32)
            for i in range(blocks):
                high, low = halves(sh_ref[i, :share, :] / STUDENT_TEMP)
                part = jnp.concatenate([high, low, jnp.zeros((LANES - 2 * share, t_rows), BF16)])
                g[i] = part
                total += mm(jnp.ones((8, t_rows), BF16), part, NT)
            g_sum[...] = total

        middle = 1.0 / (all_columns * scale_ref[...])
        wide = jnp.concatenate([middle] * tr, axis=1)
        acc = middle * g_sum[0:1, :]
        for i in range(blocks):
            scores = mm(wt_ref[...], feat_ref[i], NN)
            expo = jnp.exp2(scores * T_SCALE - offset[i : i + 1, :])
            acc += mm((expo - wide).astype(BF16), g[i], NT)
        out = (acc * scale_ref[...]).T
        out_ref[...] = out[:share] + out[share : 2 * share]

    return call(
        body,
        steps,
        [
            whole(feats.shape),
            whole(offset_packed.shape),
            whole(inverse.shape),
            pl.BlockSpec((T_CHUNK, width), lambda c: (c, 0)),
            whole(shared.shape),
            pl.BlockSpec((T_CHUNK, LANES), lambda c: (c, 0)),
        ],
        [pl.BlockSpec((share, T_CHUNK), lambda c: (0, c))],
        [struct((share, columns))],
        [
            pltpu.VMEM((max(blocks, 8), t_rows), F32),
            pltpu.VMEM((blocks, LANES, t_rows), BF16),
            pltpu.VMEM((8, LANES), F32),
        ],
        6 * columns * width * t_rows * blocks,
        columns * t_rows * blocks,
        6 * 2**20,
    )(feats, offset_packed, inverse, wt, shared, scale)[0]


def per_device(tf, sf, w, pairing):
    t_rows = tf.shape[0]
    rows = sf.shape[0]
    blocks = lax.axis_size("batch")
    peers = lax.axis_size("proto")
    me = lax.axis_index("batch").astype(jnp.int32).reshape(1)

    def swap(x, axis):
        return lax.all_to_all(x, axis, 0, 0)

    feats_f32 = lax.all_gather(turned(tf), "batch")
    pairs = pairing - me * t_rows
    onehot = (pairs[:, None] == jnp.arange(t_rows, dtype=jnp.int32)[None, :]).astype(BF16)
    wt, gt, stats = student_stats(sf, tf, w, onehot, peers)
    stats = swap(stats, "proto")
    lse, shared = merge_stats(stats, gt, rows, blocks)
    shared = swap(shared, "batch")
    ds_prob, dw_prob = student_grads(sf, w, wt, lse, peers)

    feats, offset, mass, dw_prob = first_iteration(feats_f32, shared, wt, dw_prob, peers)
    dw_prob = lax.psum_scatter(dw_prob, "batch", scatter_dimension=0, tiled=True)
    for _ in range(ITERS - 2):
        offset, mass = next_iteration(feats, offset, swap(mass, "proto"), wt)
    offset, scale, taught, mass = last_iteration(
        me, feats, offset, swap(mass, "proto"), w, wt, gt
    )
    mass = swap(mass, "proto")
    loss, inverse, ds = after_iterations(me, mass, lse, taught, onehot, ds_prob, blocks)
    ds = swap(ds, "proto")
    loss = swap(loss, "batch")
    d_weight = dw_prob - weight_grad(
        feats, offset, inverse, wt, shared, scale, w.shape[1] * peers
    )
    d_student = jnp.sum(ds, axis=0)
    loss = jnp.sum(loss[:, 0, 0]) / (rows * blocks)
    return loss, d_student, d_weight


def solution(mesh):
    placed = (P("batch", None), P("batch", None), P(None, "proto"), P("batch"))
    return jax.shard_map(
        per_device,
        mesh=mesh,
        in_specs=placed,
        out_specs=(P(), P(("batch", "proto"), None), P("batch", "proto")),
        check_vma=False,
    )
```

```python
import math

import jax
import jax.numpy as jnp
from jax import lax
from jax.experimental import pallas as pl
from jax.experimental.pallas import tpu as pltpu
from jax.sharding import PartitionSpec as P

ITERS = 3
LANES = 128
S_CHUNK = 512
T_CHUNK = 1024
TEACHER_TEMP = 0.07
STUDENT_TEMP = 0.1
LOG2E = math.log2(math.e)
T_SCALE = LOG2E / TEACHER_TEMP
S_SCALE = LOG2E / STUDENT_TEMP
F32 = jnp.float32
BF16 = jnp.bfloat16
NN = (((1,), (0,)), ((), ()))
NT = (((1,), (1,)), ((), ()))
TN = (((0,), (0,)), ((), ()))
VMEM_LIMIT = 60 * 1024 * 1024


def mm(a, b, dims):
    return lax.dot_general(a, b, dims, preferred_element_type=F32)


def halves(x):
    high = x.astype(BF16)
    return high, (x - high.astype(F32)).astype(BF16)


def by_sublane(x, combine):
    return combine(x.reshape(x.shape[0] // 8, 8, x.shape[1]), axis=0)


def whole(shape):
    return pl.BlockSpec(shape, lambda c: (0,) * len(shape))


def call(
    body, grid, in_specs, out_specs, out_shape, scratch, flops, transcendentals, size, aliases=None
):
    return pl.pallas_call(
        body,
        grid=(grid,),
        in_specs=in_specs,
        out_specs=out_specs,
        out_shape=out_shape,
        scratch_shapes=scratch,
        input_output_aliases=aliases or {},
        cost_estimate=pl.CostEstimate(
            flops=flops, transcendentals=transcendentals, bytes_accessed=size
        ),
        compiler_params=pltpu.CompilerParams(
            dimension_semantics=("arbitrary",), vmem_limit_bytes=VMEM_LIMIT
        ),
    )


def struct(shape, dtype=F32):
    return jax.ShapeDtypeStruct(shape, dtype)


def put_rows(ref, first, row):
    for i in range(row.shape[1] // LANES):
        ref[first + i : first + i + 1, :] = row[:, i * LANES : (i + 1) * LANES]


def turned(tf):
    def body(tf_ref, out_ref):
        out_ref[...] = tf_ref[...].astype(F32).T

    return call(
        body, 1, [whole(tf.shape)], [whole(tf.shape[::-1])], [struct(tf.shape[::-1])], [], 0, 0, 2**18
    )(tf)[0]


def student_stats(sf, tf, w, peers):
    rows, width = sf.shape
    t_rows = tf.shape[0]
    columns = w.shape[1]
    steps = columns // S_CHUNK
    s_rows, tr = rows // LANES, t_rows // LANES
    lines = -(-(2 * s_rows + tr) // 8) * 8

    def body(sf_ref, tf_ref, w_ref, wt_ref, out_ref, high, total, t_high, line):
        step = pl.program_id(0)

        @pl.when(step == 0)
        def _():
            high[...] = jnp.full_like(high, -3e38)
            total[...] = jnp.zeros_like(total)
            t_high[...] = jnp.full_like(t_high, -3e38)

        wt = w_ref[...].T
        wt_ref[...] = wt
        scores = mm(wt, sf_ref[...], NT)
        before = high[...]
        now = jnp.maximum(before, by_sublane(scores, jnp.max))
        high[...] = now
        groups = scores.reshape(S_CHUNK // 8, 8, rows)
        part = jnp.sum(jnp.exp2((groups - now[None]) * S_SCALE), axis=0)
        total[...] = total[...] * jnp.exp2((before - now) * S_SCALE) + part
        t_high[...] = jnp.maximum(t_high[...], by_sublane(mm(wt, tf_ref[...], NT), jnp.max))

        @pl.when(step == steps - 1)
        def _():
            best = jnp.max(high[...], axis=0, keepdims=True)
            summed = jnp.sum(
                total[...] * jnp.exp2((high[...] - best) * S_SCALE), axis=0, keepdims=True
            )
            line[...] = jnp.zeros_like(line)
            put_rows(line, 0, best)
            put_rows(line, s_rows, summed)
            put_rows(line, 2 * s_rows, jnp.max(t_high[...], axis=0, keepdims=True))
            out_ref[...] = jnp.broadcast_to(line[...][None], out_ref.shape)

    return call(
        body,
        steps,
        [
            whole(sf.shape),
            whole(tf.shape),
            pl.BlockSpec((width, S_CHUNK), lambda c: (0, c)),
        ],
        [
            pl.BlockSpec((S_CHUNK, width), lambda c: (c, 0)),
            whole((peers, lines, LANES)),
        ],
        [
            struct((columns, width), BF16),
            struct((peers, lines, LANES)),
        ],
        [
            pltpu.VMEM((8, rows), F32),
            pltpu.VMEM((8, rows), F32),
            pltpu.VMEM((8, t_rows), F32),
            pltpu.VMEM((lines, LANES), F32),
        ],
        2 * columns * width * (rows + t_rows),
        columns * rows,
        8 * 2**20,
    )(sf, tf, w)


def merge_stats(stats, gt, rows, batches):
    width, t_rows = gt.shape
    share = width // batches
    s_rows, tr = rows // LANES, t_rows // LANES

    def body(stats_ref, gt_ref, lse_ref, out_ref):
        highs = stats_ref[:, :s_rows, :]
        best = jnp.max(highs, axis=0)
        total = jnp.sum(
            stats_ref[:, s_rows : 2 * s_rows, :] * jnp.exp2((highs - best[None]) * S_SCALE), axis=0
        )
        lse_ref[...] = best * S_SCALE + jnp.log2(total)
        t_best = jnp.max(stats_ref[:, 2 * s_rows : 2 * s_rows + tr, :], axis=0) * T_SCALE
        row = jnp.concatenate([t_best[i : i + 1, :] for i in range(tr)], axis=1)
        for b in range(batches):
            out_ref[b, :share, :] = gt_ref[b * share : (b + 1) * share, :]
            out_ref[b, share:, :] = jnp.broadcast_to(row, (8, t_rows))

    return call(
        body,
        1,
        [whole(stats.shape), whole(gt.shape)],
        [whole((s_rows, LANES)), whole((batches, share + 8, t_rows))],
        [struct((s_rows, LANES)), struct((batches, share + 8, t_rows))],
        [],
        stats.size * 4,
        stats.size,
        2**21,
    )(stats, gt)


def student_grads(sf, w, wt, lse, half, before, peers):
    rows, width = sf.shape
    columns = w.shape[1]
    steps = columns // S_CHUNK // 2
    first = half * steps
    s_rows = rows // LANES

    def body(sf_ref, w_ref, wt_ref, lse_ref, *rest):
        if half:
            _, old_ref, ds_ref, dw_ref, lse_row, sft, acc = rest
        else:
            ds_ref, dw_ref, lse_row, sft, acc = rest
        step = pl.program_id(0)

        @pl.when(step == 0)
        def _():
            for i in range(s_rows):
                lse_row[:, i * LANES : (i + 1) * LANES] = lse_ref[i : i + 1, :]
            sft[...] = sf_ref[...].T
            acc[...] = old_ref[...] if half else jnp.zeros_like(acc)

        scores = mm(wt_ref[...], sf_ref[...], NT)
        high, low = halves(jnp.exp2(scores * S_SCALE - lse_row[...]))
        acc[...] += mm(w_ref[...], high, NN) + mm(w_ref[...], low, NN)
        dw_ref[...] = (mm(sft[...], high, NT) + mm(sft[...], low, NT)) / STUDENT_TEMP

        @pl.when(step == steps - 1)
        def _():
            if half:
                ds_ref[...] = (acc[...].T / STUDENT_TEMP).reshape(ds_ref.shape)
            else:
                ds_ref[...] = acc[...]

    ds_shape = (peers, rows // peers, width) if half else (width, rows)
    in_specs = [
        whole(sf.shape),
        pl.BlockSpec((width, S_CHUNK), lambda c: (0, c + first)),
        pl.BlockSpec((S_CHUNK, width), lambda c: (c + first, 0)),
        whole(lse.shape),
    ]
    operands = [sf, w, wt, lse]
    if half:
        in_specs += [pl.BlockSpec(memory_space=pl.ANY), whole((width, rows))]
        operands += [before[1], before[0]]
    return call(
        body,
        steps,
        in_specs,
        [whole(ds_shape), pl.BlockSpec((width, S_CHUNK), lambda c: (0, c + first))],
        [struct(ds_shape), struct((width, columns))],
        [
            pltpu.VMEM((1, rows), F32),
            pltpu.VMEM((width, rows), BF16),
            pltpu.VMEM((width, rows), F32),
        ],
        8 * columns * width * rows,
        columns * rows // 2,
        6 * 2**20,
        {4: 1} if half else None,
    )(*operands)


def fill_offsets(offset, packed, blocks, per_block):
    for i in range(blocks):
        for j in range(per_block):
            line = i * per_block + j
            offset[i : i + 1, j * LANES : (j + 1) * LANES] = packed[line : line + 1, :]


def expos_and_scale(wt, feats, offset, expo, blocks, all_columns):
    partial = None
    for i in range(blocks):
        scores = mm(wt, feats[i], NN)
        values = jnp.exp2(scores * T_SCALE - offset[i : i + 1, :])
        expo[i] = values
        for j in range(values.shape[1] // LANES):
            piece = values[:, j * LANES : (j + 1) * LANES]
            partial = piece if partial is None else partial + piece
    return 1.0 / (all_columns * jnp.sum(partial, axis=1, keepdims=True))


def add_rows(expo, scale, mass, blocks):
    for i in range(blocks):
        mass[i] += by_sublane(expo[i] * scale, jnp.sum)


def put_mass(mass, line, blocks):
    for i in range(blocks):
        row = jnp.sum(mass[i], axis=0, keepdims=True)
        put_rows(line, i * (row.shape[1] // LANES), row)


def first_iteration(feats_f32, shared, wt, passed, peers):
    blocks, width, t_rows = feats_f32.shape
    columns = wt.shape[0]
    steps = columns // T_CHUNK
    tr = t_rows // LANES
    share = shared.shape[1] - 8

    def body(
        feat_ref, shared_ref, wt_ref, _,
        feat_out, off_out, out_ref, __, offset, expo, mass, line,
    ):
        step = pl.program_id(0)

        @pl.when(step == 0)
        def _():
            feat_out[...] = feat_ref[...].astype(BF16)
            for i in range(blocks):
                row = shared_ref[i, share : share + 1, :]
                offset[i : i + 1, :] = row
                put_rows(off_out, i * tr, row)
            mass[...] = jnp.zeros_like(mass)

        scale = expos_and_scale(wt_ref[...], feat_out, offset, expo, blocks, columns * peers)
        add_rows(expo, scale, mass, blocks)

        @pl.when(step == steps - 1)
        def _():
            put_mass(mass, line, blocks)
            out_ref[...] = jnp.broadcast_to(line[...][None], out_ref.shape)

    return call(
        body,
        steps,
        [
            whole(feats_f32.shape),
            whole(shared.shape),
            pl.BlockSpec((T_CHUNK, width), lambda c: (c, 0)),
            pl.BlockSpec(memory_space=pl.ANY),
        ],
        [
            whole(feats_f32.shape),
            whole((blocks * tr, LANES)),
            whole((peers, blocks * tr, LANES)),
            pl.BlockSpec(memory_space=pl.ANY),
        ],
        [
            struct(feats_f32.shape, BF16),
            struct((blocks * tr, LANES)),
            struct((peers, blocks * tr, LANES)),
            struct(passed.shape),
        ],
        [
            pltpu.VMEM((max(blocks, 8), t_rows), F32),
            pltpu.VMEM((blocks, T_CHUNK, t_rows), F32),
            pltpu.VMEM((blocks, 8, t_rows), F32),
            pltpu.VMEM((blocks * tr, LANES), F32),
        ],
        5 * columns * width * t_rows * blocks,
        columns * t_rows * blocks,
        5 * 2**20,
        {3: 3},
    )(feats_f32, shared, wt, passed)


def next_iteration(feats, old, received, wt, passed):
    blocks, width, t_rows = feats.shape
    columns = wt.shape[0]
    peers = received.shape[0]
    steps = columns // T_CHUNK
    tr = t_rows // LANES
    total_t = blocks * t_rows

    def body(
        feat_ref, old_ref, recv_ref, wt_ref, _,
        off_out, out_ref, __, offset, expo, mass, line,
    ):
        step = pl.program_id(0)

        @pl.when(step == 0)
        def _():
            packed = old_ref[...] + jnp.log2(total_t * jnp.sum(recv_ref[...], axis=0))
            off_out[...] = packed
            fill_offsets(offset, packed, blocks, tr)
            mass[...] = jnp.zeros_like(mass)

        scale = expos_and_scale(wt_ref[...], feat_ref, offset, expo, blocks, columns * peers)
        add_rows(expo, scale, mass, blocks)

        @pl.when(step == steps - 1)
        def _():
            put_mass(mass, line, blocks)
            out_ref[...] = jnp.broadcast_to(line[...][None], out_ref.shape)

    return call(
        body,
        steps,
        [
            whole(feats.shape),
            whole(old.shape),
            whole(received.shape),
            pl.BlockSpec((T_CHUNK, width), lambda c: (c, 0)),
            pl.BlockSpec(memory_space=pl.ANY),
        ],
        [
            whole(old.shape),
            whole((peers, blocks * tr, LANES)),
            pl.BlockSpec(memory_space=pl.ANY),
        ],
        [struct(old.shape), struct((peers, blocks * tr, LANES)), struct(passed.shape)],
        [
            pltpu.VMEM((max(blocks, 8), t_rows), F32),
            pltpu.VMEM((blocks, T_CHUNK, t_rows), F32),
            pltpu.VMEM((blocks, 8, t_rows), F32),
            pltpu.VMEM((blocks * tr, LANES), F32),
        ],
        5 * columns * width * t_rows * blocks,
        columns * t_rows * blocks,
        4 * 2**20,
        {4: 2},
    )(feats, old, received, wt, passed)


def last_iteration(me, feats, old, received, w, wt, gt):
    blocks, width, t_rows = feats.shape
    columns = wt.shape[0]
    peers = received.shape[0]
    steps = columns // T_CHUNK
    tr = t_rows // LANES
    total_t = blocks * t_rows
    lines = -(-(blocks * tr + tr) // 8) * 8

    def body(
        me_ref, feat_ref, old_ref, recv_ref, w_ref, wt_ref, gt_ref,
        off_out, scale_out, taught_ref, out_ref, offset, expo, mass, line, acc, w_last, high, low,
    ):
        step = pl.program_id(0)

        @pl.when(step == 0)
        def _():
            packed = old_ref[...] + jnp.log2(total_t * jnp.sum(recv_ref[...], axis=0))
            off_out[...] = packed
            fill_offsets(offset, packed, blocks, tr)
            mass[...] = jnp.zeros_like(mass)
            acc[...] = jnp.zeros_like(acc)
            w_last[...] = jnp.zeros_like(w_last)
            high[...] = jnp.zeros_like(high)
            low[...] = jnp.zeros_like(low)

        def add_taught():
            acc[...] += mm(w_last[...], high[...], NN) + mm(w_last[...], low[...], NN)

        scale = expos_and_scale(wt_ref[...], feat_ref, offset, expo, blocks, columns * peers)
        scale_out[...] = jnp.broadcast_to(scale, scale_out.shape)
        add_taught()
        add_rows(expo, scale, mass, blocks)
        high[...], low[...] = halves(expo[me_ref[0]] * scale)
        w_last[...] = w_ref[...]

        @pl.when(step == steps - 1)
        def _():
            add_taught()
            line[...] = jnp.zeros_like(line)
            put_mass(mass, line, blocks)
            put_rows(line, blocks * tr, jnp.sum(acc[...] * gt_ref[...], axis=0, keepdims=True))
            out_ref[...] = jnp.broadcast_to(line[...][None], out_ref.shape)
            taught_ref[...] = acc[...]

    return call(
        body,
        steps,
        [
            pl.BlockSpec(memory_space=pltpu.SMEM),
            whole(feats.shape),
            whole(old.shape),
            whole(received.shape),
            pl.BlockSpec((width, T_CHUNK), lambda c: (0, c)),
            pl.BlockSpec((T_CHUNK, width), lambda c: (c, 0)),
            whole(gt.shape),
        ],
        [
            whole(old.shape),
            pl.BlockSpec((T_CHUNK, LANES), lambda c: (c, 0)),
            whole((width, t_rows)),
            whole((peers, lines, LANES)),
        ],
        [
            struct(old.shape),
            struct((columns, LANES)),
            struct((width, t_rows)),
            struct((peers, lines, LANES)),
        ],
        [
            pltpu.VMEM((max(blocks, 8), t_rows), F32),
            pltpu.VMEM((blocks, T_CHUNK, t_rows), F32),
            pltpu.VMEM((blocks, 8, t_rows), F32),
            pltpu.VMEM((lines, LANES), F32),
            pltpu.VMEM((width, t_rows), F32),
            pltpu.VMEM((width, T_CHUNK), BF16),
            pltpu.VMEM((T_CHUNK, t_rows), BF16),
            pltpu.VMEM((T_CHUNK, t_rows), BF16),
        ],
        2 * columns * width * t_rows * (blocks + 2),
        columns * t_rows * blocks,
        8 * 2**20,
    )(me, feats, old, received, w, wt, gt)


def after_iterations(me, received, lse, taught, onehot, ds_prob, blocks):
    width, t_rows = taught.shape
    tr = t_rows // LANES
    n = blocks * tr

    def body(me_ref, recv_ref, lse_ref, taught_ref, oh_ref, prob_ref, part_ref, inv_ref, ds_ref):
        total = jnp.sum(recv_ref[...], axis=0)
        inv_ref[...] = 1.0 / total[:n]
        start = me_ref[0] * tr
        inverse = 1.0 / jnp.sum(recv_ref[:, pl.ds(start, tr), :], axis=0)
        product = jnp.sum(total[n : n + tr] * inverse) / STUDENT_TEMP
        part_ref[...] = jnp.full(part_ref.shape, jnp.sum(lse_ref[...]) / LOG2E - product, F32)
        row = jnp.concatenate([inverse[i : i + 1, :] for i in range(tr)], axis=1)
        high, low = halves(taught_ref[...] * row / STUDENT_TEMP)
        wanted = mm(oh_ref[...], high, NT) + mm(oh_ref[...], low, NT)
        ds_ref[...] = prob_ref[...] - wanted.reshape(ds_ref.shape)

    return call(
        body,
        1,
        [
            pl.BlockSpec(memory_space=pltpu.SMEM),
            whole(received.shape),
            whole(lse.shape),
            whole(taught.shape),
            whole(onehot.shape),
            whole(ds_prob.shape),
        ],
        [whole((8, LANES)), whole((n, LANES)), whole(ds_prob.shape)],
        [struct((8, LANES)), struct((n, LANES)), struct(ds_prob.shape)],
        [],
        4 * onehot.size * width,
        1024,
        3 * 2**20,
    )(me, received, lse, taught, onehot, ds_prob)


def weight_grad(feats, offset_packed, inverse, wt, shared, scale, all_columns):
    blocks, width, t_rows = feats.shape
    columns = wt.shape[0]
    steps = columns // T_CHUNK
    tr = t_rows // LANES
    share = shared.shape[1] - 8

    def body(feat_ref, off_ref, inv_ref, wt_ref, sh_ref, scale_ref, out_ref, offset, g, g_sum):
        @pl.when(pl.program_id(0) == 0)
        def _():
            fill_offsets(offset, off_ref[...] - jnp.log2(inv_ref[...]), blocks, tr)
            total = jnp.zeros((8, LANES), F32)
            for i in range(blocks):
                high, low = halves(sh_ref[i, :share, :] / STUDENT_TEMP)
                part = jnp.concatenate([high, low, jnp.zeros((LANES - 2 * share, t_rows), BF16)])
                g[i] = part
                total += mm(jnp.ones((8, t_rows), BF16), part, NT)
            g_sum[...] = total

        middle = 1.0 / (all_columns * scale_ref[...])
        wide = jnp.concatenate([middle] * tr, axis=1)
        acc = middle * g_sum[0:1, :]
        for i in range(blocks):
            scores = mm(wt_ref[...], feat_ref[i], NN)
            expo = jnp.exp2(scores * T_SCALE - offset[i : i + 1, :])
            acc += mm((expo - wide).astype(BF16), g[i], NT)
        out = (acc * scale_ref[...]).T
        out_ref[...] = out[:share] + out[share : 2 * share]

    return call(
        body,
        steps,
        [
            whole(feats.shape),
            whole(offset_packed.shape),
            whole(inverse.shape),
            pl.BlockSpec((T_CHUNK, width), lambda c: (c, 0)),
            whole(shared.shape),
            pl.BlockSpec((T_CHUNK, LANES), lambda c: (c, 0)),
        ],
        [pl.BlockSpec((share, T_CHUNK), lambda c: (0, c))],
        [struct((share, columns))],
        [
            pltpu.VMEM((max(blocks, 8), t_rows), F32),
            pltpu.VMEM((blocks, LANES, t_rows), BF16),
            pltpu.VMEM((8, LANES), F32),
        ],
        6 * columns * width * t_rows * blocks,
        columns * t_rows * blocks,
        6 * 2**20,
    )(feats, offset_packed, inverse, wt, shared, scale)[0]


def per_device(tf, sf, w, pairing):
    t_rows = tf.shape[0]
    rows = sf.shape[0]
    blocks = lax.axis_size("batch")
    peers = lax.axis_size("proto")
    me = lax.axis_index("batch").astype(jnp.int32).reshape(1)

    def swap(x, axis):
        return lax.all_to_all(x, axis, 0, 0)

    feats_f32 = lax.all_gather(turned(tf), "batch")
    pairs = pairing - me * t_rows
    onehot = (pairs[:, None] == jnp.arange(t_rows, dtype=jnp.int32)[None, :]).astype(BF16)
    gt = mm(sf, onehot, TN)
    wt, stats = student_stats(sf, tf, w, peers)
    stats = swap(stats, "proto")
    lse, shared = merge_stats(stats, gt, rows, blocks)
    shared = swap(shared, "batch")
    ds_prob, dw_prob = student_grads(sf, w, wt, lse, 0, None, peers)

    feats, offset, mass, dw_prob = first_iteration(feats_f32, shared, wt, dw_prob, peers)
    ds_prob, dw_prob = student_grads(sf, w, wt, lse, 1, (ds_prob, dw_prob), peers)
    for _ in range(ITERS - 2):
        offset, mass, dw_prob = next_iteration(feats, offset, swap(mass, "proto"), wt, dw_prob)
    dw_prob = lax.psum_scatter(dw_prob, "batch", scatter_dimension=0, tiled=True)
    offset, scale, taught, mass = last_iteration(
        me, feats, offset, swap(mass, "proto"), w, wt, gt
    )
    mass = swap(mass, "proto")
    loss, inverse, ds = after_iterations(me, mass, lse, taught, onehot, ds_prob, blocks)
    ds = swap(ds, "proto")
    far = 1
    while far < blocks:
        loss = loss + lax.ppermute(loss, "batch", [(i, i ^ far) for i in range(blocks)])
        far *= 2
    d_weight = dw_prob - weight_grad(
        feats, offset, inverse, wt, shared, scale, w.shape[1] * peers
    )
    return loss[0, 0] / (rows * blocks), jnp.sum(ds, axis=0), d_weight


def solution(mesh):
    placed = (P("batch", None), P("batch", None), P(None, "proto"), P("batch"))
    return jax.shard_map(
        per_device,
        mesh=mesh,
        in_specs=placed,
        out_specs=(P(), P(("batch", "proto"), None), P("batch", "proto")),
        check_vma=False,
    )
```

```python
import math

import jax
import jax.numpy as jnp
from jax import lax
from jax.experimental import pallas as pl
from jax.experimental.pallas import tpu as pltpu
from jax.sharding import PartitionSpec as P

ITERS = 3
LANES = 128
S_CHUNK = 512
T_CHUNK = 1024
TEACHER_TEMP = 0.07
STUDENT_TEMP = 0.1
LOG2E = math.log2(math.e)
T_SCALE = LOG2E / TEACHER_TEMP
S_SCALE = LOG2E / STUDENT_TEMP
F32 = jnp.float32
BF16 = jnp.bfloat16
NN = (((1,), (0,)), ((), ()))
NT = (((1,), (1,)), ((), ()))
TN = (((0,), (0,)), ((), ()))
VMEM_LIMIT = 56 * 1024 * 1024


def mm(a, b, dims):
    return lax.dot_general(a, b, dims, preferred_element_type=F32)


def halves(x):
    high = x.astype(BF16)
    return high, (x - high.astype(F32)).astype(BF16)


def by_sublane(x, combine):
    return combine(x.reshape(x.shape[0] // 8, 8, x.shape[1]), axis=0)


def whole(shape):
    return pl.BlockSpec(shape, lambda c: (0,) * len(shape))


def call(
    body, grid, in_specs, out_specs, out_shape, scratch, flops, transcendentals, size, aliases=None
):
    return pl.pallas_call(
        body,
        grid=(grid,),
        in_specs=in_specs,
        out_specs=out_specs,
        out_shape=out_shape,
        scratch_shapes=scratch,
        input_output_aliases=aliases or {},
        cost_estimate=pl.CostEstimate(
            flops=flops, transcendentals=transcendentals, bytes_accessed=size
        ),
        compiler_params=pltpu.CompilerParams(
            dimension_semantics=("arbitrary",), vmem_limit_bytes=VMEM_LIMIT
        ),
    )


def struct(shape, dtype=F32):
    return jax.ShapeDtypeStruct(shape, dtype)


def put_rows(ref, first, row):
    for i in range(row.shape[1] // LANES):
        ref[first + i : first + i + 1, :] = row[:, i * LANES : (i + 1) * LANES]


def turned(tf):
    def body(tf_ref, out_ref):
        out_ref[...] = tf_ref[...].astype(F32).T

    return call(
        body, 1, [whole(tf.shape)], [whole(tf.shape[::-1])], [struct(tf.shape[::-1])], [], 0, 0, 2**18
    )(tf)[0]


def student_stats(sf, tf, w, peers):
    rows, width = sf.shape
    t_rows = tf.shape[0]
    columns = w.shape[1]
    steps = columns // S_CHUNK
    s_rows, tr = rows // LANES, t_rows // LANES
    lines = -(-(2 * s_rows + tr) // 8) * 8

    def body(sf_ref, tf_ref, w_ref, wt_ref, out_ref, high, total, t_high, line):
        step = pl.program_id(0)

        @pl.when(step == 0)
        def _():
            high[...] = jnp.full_like(high, -3e38)
            total[...] = jnp.zeros_like(total)
            t_high[...] = jnp.full_like(t_high, -3e38)

        wt = w_ref[...].T
        wt_ref[...] = wt
        scores = mm(wt, sf_ref[...], NT)
        before = high[...]
        now = jnp.maximum(before, by_sublane(scores, jnp.max))
        high[...] = now
        groups = scores.reshape(S_CHUNK // 8, 8, rows)
        part = jnp.sum(jnp.exp2((groups - now[None]) * S_SCALE), axis=0)
        total[...] = total[...] * jnp.exp2((before - now) * S_SCALE) + part
        t_high[...] = jnp.maximum(t_high[...], by_sublane(mm(wt, tf_ref[...], NT), jnp.max))

        @pl.when(step == steps - 1)
        def _():
            best = jnp.max(high[...], axis=0, keepdims=True)
            summed = jnp.sum(
                total[...] * jnp.exp2((high[...] - best) * S_SCALE), axis=0, keepdims=True
            )
            line[...] = jnp.zeros_like(line)
            put_rows(line, 0, best)
            put_rows(line, s_rows, summed)
            put_rows(line, 2 * s_rows, jnp.max(t_high[...], axis=0, keepdims=True))
            out_ref[...] = jnp.broadcast_to(line[...][None], out_ref.shape)

    return call(
        body,
        steps,
        [
            whole(sf.shape),
            whole(tf.shape),
            pl.BlockSpec((width, S_CHUNK), lambda c: (0, c)),
        ],
        [
            pl.BlockSpec((S_CHUNK, width), lambda c: (c, 0)),
            whole((peers, lines, LANES)),
        ],
        [
            struct((columns, width), BF16),
            struct((peers, lines, LANES)),
        ],
        [
            pltpu.VMEM((8, rows), F32),
            pltpu.VMEM((8, rows), F32),
            pltpu.VMEM((8, t_rows), F32),
            pltpu.VMEM((lines, LANES), F32),
        ],
        2 * columns * width * (rows + t_rows),
        columns * rows,
        8 * 2**20,
    )(sf, tf, w)


def merge_stats(stats, gt, rows, batches):
    width, t_rows = gt.shape
    share = width // batches
    s_rows, tr = rows // LANES, t_rows // LANES

    def body(stats_ref, gt_ref, lse_ref, out_ref):
        highs = stats_ref[:, :s_rows, :]
        best = jnp.max(highs, axis=0)
        total = jnp.sum(
            stats_ref[:, s_rows : 2 * s_rows, :] * jnp.exp2((highs - best[None]) * S_SCALE), axis=0
        )
        lse_ref[...] = best * S_SCALE + jnp.log2(total)
        t_best = jnp.max(stats_ref[:, 2 * s_rows : 2 * s_rows + tr, :], axis=0) * T_SCALE
        row = jnp.concatenate([t_best[i : i + 1, :] for i in range(tr)], axis=1)
        for b in range(batches):
            out_ref[b, :share, :] = gt_ref[b * share : (b + 1) * share, :]
            out_ref[b, share:, :] = jnp.broadcast_to(row, (8, t_rows))

    return call(
        body,
        1,
        [whole(stats.shape), whole(gt.shape)],
        [whole((s_rows, LANES)), whole((batches, share + 8, t_rows))],
        [struct((s_rows, LANES)), struct((batches, share + 8, t_rows))],
        [],
        stats.size * 4,
        stats.size,
        2**21,
    )(stats, gt)


def student_grads(sf, w, wt, lse, half, before, peers):
    rows, width = sf.shape
    columns = w.shape[1]
    all_steps = columns // S_CHUNK
    cut = (5 * all_steps) // 8
    steps = all_steps - cut if half else cut
    first = half * cut
    s_rows = rows // LANES

    def body(sf_ref, w_ref, wt_ref, lse_ref, *rest):
        if half:
            _, old_ref, ds_ref, dw_ref, lse_row, sft, acc = rest
        else:
            ds_ref, dw_ref, lse_row, sft, acc = rest
        step = pl.program_id(0)

        @pl.when(step == 0)
        def _():
            for i in range(s_rows):
                lse_row[:, i * LANES : (i + 1) * LANES] = lse_ref[i : i + 1, :]
            sft[...] = sf_ref[...].T
            acc[...] = old_ref[...] if half else jnp.zeros_like(acc)

        scores = mm(wt_ref[...], sf_ref[...], NT)
        high, low = halves(jnp.exp2(scores * S_SCALE - lse_row[...]))
        acc[...] += mm(w_ref[...], high, NN) + mm(w_ref[...], low, NN)
        dw_ref[...] = (mm(sft[...], high, NT) + mm(sft[...], low, NT)) / STUDENT_TEMP

        @pl.when(step == steps - 1)
        def _():
            if half:
                ds_ref[...] = (acc[...].T / STUDENT_TEMP).reshape(ds_ref.shape)
            else:
                ds_ref[...] = acc[...]

    ds_shape = (peers, rows // peers, width) if half else (width, rows)
    in_specs = [
        whole(sf.shape),
        pl.BlockSpec((width, S_CHUNK), lambda c: (0, c + first)),
        pl.BlockSpec((S_CHUNK, width), lambda c: (c + first, 0)),
        whole(lse.shape),
    ]
    operands = [sf, w, wt, lse]
    if half:
        in_specs += [pl.BlockSpec(memory_space=pl.ANY), whole((width, rows))]
        operands += [before[1], before[0]]
    return call(
        body,
        steps,
        in_specs,
        [whole(ds_shape), pl.BlockSpec((width, S_CHUNK), lambda c: (0, c + first))],
        [struct(ds_shape), struct((width, columns))],
        [
            pltpu.VMEM((1, rows), F32),
            pltpu.VMEM((width, rows), BF16),
            pltpu.VMEM((width, rows), F32),
        ],
        16 * columns * width * rows * steps // all_steps,
        columns * rows // 2,
        6 * 2**20,
        {4: 1} if half else None,
    )(*operands)


def fill_offsets(offset, packed, blocks, per_block):
    for i in range(blocks):
        for j in range(per_block):
            line = i * per_block + j
            offset[i : i + 1, j * LANES : (j + 1) * LANES] = packed[line : line + 1, :]


def expos_and_scale(wt, feats, offset, expo, blocks, all_columns):
    partial = None
    for i in range(blocks):
        scores = mm(wt, feats[i], NN)
        values = jnp.exp2(scores * T_SCALE - offset[i : i + 1, :])
        expo[i] = values
        for j in range(values.shape[1] // LANES):
            piece = values[:, j * LANES : (j + 1) * LANES]
            partial = piece if partial is None else partial + piece
    return 1.0 / (all_columns * jnp.sum(partial, axis=1, keepdims=True))


def add_rows(expo, scale, mass, blocks):
    for i in range(blocks):
        mass[i] += by_sublane(expo[i] * scale, jnp.sum)


def put_mass(mass, line, blocks):
    for i in range(blocks):
        row = jnp.sum(mass[i], axis=0, keepdims=True)
        put_rows(line, i * (row.shape[1] // LANES), row)


def first_iteration(feats_f32, shared, wt, passed, peers):
    blocks, width, t_rows = feats_f32.shape
    columns = wt.shape[0]
    steps = columns // T_CHUNK
    tr = t_rows // LANES
    share = shared.shape[1] - 8

    def body(
        feat_ref, shared_ref, wt_ref, _,
        feat_out, off_out, out_ref, __, offset, expo, mass, line,
    ):
        step = pl.program_id(0)

        @pl.when(step == 0)
        def _():
            feat_out[...] = feat_ref[...].astype(BF16)
            for i in range(blocks):
                row = shared_ref[i, 0:1, :]
                offset[i : i + 1, :] = row
                put_rows(off_out, i * tr, row)
            mass[...] = jnp.zeros_like(mass)

        scale = expos_and_scale(wt_ref[...], feat_out, offset, expo, blocks, columns * peers)
        add_rows(expo, scale, mass, blocks)

        @pl.when(step == steps - 1)
        def _():
            put_mass(mass, line, blocks)
            out_ref[...] = jnp.broadcast_to(line[...][None], out_ref.shape)

    return call(
        body,
        steps,
        [
            whole(feats_f32.shape),
            pl.BlockSpec((blocks, 8, t_rows), lambda c: (0, share // 8, 0)),
            pl.BlockSpec((T_CHUNK, width), lambda c: (c, 0)),
            pl.BlockSpec(memory_space=pl.ANY),
        ],
        [
            whole(feats_f32.shape),
            whole((blocks * tr, LANES)),
            whole((peers, blocks * tr, LANES)),
            pl.BlockSpec(memory_space=pl.ANY),
        ],
        [
            struct(feats_f32.shape, BF16),
            struct((blocks * tr, LANES)),
            struct((peers, blocks * tr, LANES)),
            struct(passed.shape),
        ],
        [
            pltpu.VMEM((max(blocks, 8), t_rows), F32),
            pltpu.VMEM((blocks, T_CHUNK, t_rows), F32),
            pltpu.VMEM((blocks, 8, t_rows), F32),
            pltpu.VMEM((blocks * tr, LANES), F32),
        ],
        5 * columns * width * t_rows * blocks,
        columns * t_rows * blocks,
        5 * 2**20,
        {3: 3},
    )(feats_f32, shared, wt, passed)


def next_iteration(feats, old, received, wt, passed, peers):
    blocks, width, t_rows = feats.shape
    columns = wt.shape[0]
    steps = columns // T_CHUNK
    tr = t_rows // LANES
    total_t = blocks * t_rows

    def body(
        feat_ref, old_ref, recv_ref, wt_ref, _,
        off_out, out_ref, __, offset, expo, mass, line,
    ):
        step = pl.program_id(0)

        @pl.when(step == 0)
        def _():
            packed = old_ref[...] + jnp.log2(total_t * recv_ref[...])
            off_out[...] = packed
            fill_offsets(offset, packed, blocks, tr)
            mass[...] = jnp.zeros_like(mass)

        scale = expos_and_scale(wt_ref[...], feat_ref, offset, expo, blocks, columns * peers)
        add_rows(expo, scale, mass, blocks)

        @pl.when(step == steps - 1)
        def _():
            put_mass(mass, line, blocks)
            out_ref[...] = jnp.broadcast_to(line[...][None], out_ref.shape)

    return call(
        body,
        steps,
        [
            whole(feats.shape),
            whole(old.shape),
            whole(received.shape),
            pl.BlockSpec((T_CHUNK, width), lambda c: (c, 0)),
            pl.BlockSpec(memory_space=pl.ANY),
        ],
        [
            whole(old.shape),
            whole((peers, blocks * tr, LANES)),
            pl.BlockSpec(memory_space=pl.ANY),
        ],
        [struct(old.shape), struct((peers, blocks * tr, LANES)), struct(passed.shape)],
        [
            pltpu.VMEM((max(blocks, 8), t_rows), F32),
            pltpu.VMEM((blocks, T_CHUNK, t_rows), F32),
            pltpu.VMEM((blocks, 8, t_rows), F32),
            pltpu.VMEM((blocks * tr, LANES), F32),
        ],
        5 * columns * width * t_rows * blocks,
        columns * t_rows * blocks,
        4 * 2**20,
        {4: 2},
    )(feats, old, received, wt, passed)


def last_iteration(me, feats, old, received, w, wt, gt, peers):
    blocks, width, t_rows = feats.shape
    columns = wt.shape[0]
    steps = columns // T_CHUNK
    tr = t_rows // LANES
    total_t = blocks * t_rows
    lines = -(-(blocks * tr + tr) // 8) * 8

    def body(
        me_ref, feat_ref, old_ref, recv_ref, w_ref, wt_ref, gt_ref,
        off_out, scale_out, taught_ref, out_ref, offset, expo, mass, line, acc, w_last, high, low,
    ):
        step = pl.program_id(0)

        @pl.when(step == 0)
        def _():
            packed = old_ref[...] + jnp.log2(total_t * recv_ref[...])
            off_out[...] = packed
            fill_offsets(offset, packed, blocks, tr)
            mass[...] = jnp.zeros_like(mass)
            acc[...] = jnp.zeros_like(acc)
            w_last[...] = jnp.zeros_like(w_last)
            high[...] = jnp.zeros_like(high)
            low[...] = jnp.zeros_like(low)

        def add_taught():
            acc[...] += mm(w_last[...], high[...], NN) + mm(w_last[...], low[...], NN)

        scale = expos_and_scale(wt_ref[...], feat_ref, offset, expo, blocks, columns * peers)
        scale_out[...] = jnp.broadcast_to(scale, scale_out.shape)
        add_taught()
        add_rows(expo, scale, mass, blocks)
        high[...], low[...] = halves(expo[me_ref[0]] * scale)
        w_last[...] = w_ref[...]

        @pl.when(step == steps - 1)
        def _():
            add_taught()
            line[...] = jnp.zeros_like(line)
            put_mass(mass, line, blocks)
            put_rows(line, blocks * tr, jnp.sum(acc[...] * gt_ref[...], axis=0, keepdims=True))
            out_ref[...] = jnp.broadcast_to(line[...][None], out_ref.shape)
            taught_ref[...] = acc[...]

    return call(
        body,
        steps,
        [
            pl.BlockSpec(memory_space=pltpu.SMEM),
            whole(feats.shape),
            whole(old.shape),
            whole(received.shape),
            pl.BlockSpec((width, T_CHUNK), lambda c: (0, c)),
            pl.BlockSpec((T_CHUNK, width), lambda c: (c, 0)),
            whole(gt.shape),
        ],
        [
            whole(old.shape),
            pl.BlockSpec((T_CHUNK, LANES), lambda c: (c, 0)),
            whole((width, t_rows)),
            whole((peers, lines, LANES)),
        ],
        [
            struct(old.shape),
            struct((columns, LANES)),
            struct((width, t_rows)),
            struct((peers, lines, LANES)),
        ],
        [
            pltpu.VMEM((max(blocks, 8), t_rows), F32),
            pltpu.VMEM((blocks, T_CHUNK, t_rows), F32),
            pltpu.VMEM((blocks, 8, t_rows), F32),
            pltpu.VMEM((lines, LANES), F32),
            pltpu.VMEM((width, t_rows), F32),
            pltpu.VMEM((width, T_CHUNK), BF16),
            pltpu.VMEM((T_CHUNK, t_rows), BF16),
            pltpu.VMEM((T_CHUNK, t_rows), BF16),
        ],
        2 * columns * width * t_rows * (blocks + 2),
        columns * t_rows * blocks,
        8 * 2**20,
    )(me, feats, old, received, w, wt, gt)


def after_iterations(me, received, lse, taught, onehot, ds_prob, near, blocks):
    width, t_rows = taught.shape
    tr = t_rows // LANES
    n = blocks * tr

    def body(
        me_ref, recv_ref, lse_ref, taught_ref, oh_ref, prob_ref, _, part_ref, inv_ref, ds_ref
    ):
        inv_ref[...] = 1.0 / recv_ref[:n, :]
        inverse = inv_ref[pl.ds(me_ref[0] * tr, tr), :]
        product = jnp.sum(recv_ref[n : n + tr, :] * inverse) / STUDENT_TEMP
        part_ref[...] = jnp.full(part_ref.shape, jnp.sum(lse_ref[...]) / LOG2E - product, F32)
        row = jnp.concatenate([inverse[i : i + 1, :] for i in range(tr)], axis=1)
        high, low = halves(taught_ref[...] * row / STUDENT_TEMP)
        wanted = mm(oh_ref[...], high, NT) + mm(oh_ref[...], low, NT)
        ds_ref[...] = prob_ref[...] - wanted.reshape(ds_ref.shape)

    return call(
        body,
        1,
        [
            pl.BlockSpec(memory_space=pltpu.SMEM),
            whole(received.shape),
            whole(lse.shape),
            whole(taught.shape),
            whole(onehot.shape),
            whole(ds_prob.shape),
            pl.BlockSpec(memory_space=pl.ANY),
        ],
        [whole((8, LANES)), whole((n, LANES)), whole(ds_prob.shape)],
        [struct((8, LANES)), struct((n, LANES)), struct(ds_prob.shape)],
        [],
        4 * onehot.size * width,
        1024,
        3 * 2**20,
    )(me, received, lse, taught, onehot, ds_prob, near)


def middle_of(scale_ref, all_columns, total_t, tr):
    middle = 1.0 / (all_columns * total_t * scale_ref)
    return middle, jnp.concatenate([middle] * tr, axis=1)


def early_expos(feats, offset_packed, wt, scale, all_columns):
    blocks, width, t_rows = feats.shape
    columns = wt.shape[0]
    half = T_CHUNK // 2
    steps = columns // T_CHUNK
    tr = t_rows // LANES

    def body(feat_ref, off_ref, wt_ref, scale_ref, out_ref, offset):
        @pl.when(pl.program_id(0) == 0)
        def _():
            fill_offsets(offset, off_ref[...], blocks, tr)

        _, wide = middle_of(scale_ref[...], all_columns, blocks * t_rows, tr)
        for i in range(blocks):
            scores = mm(wt_ref[...], feat_ref[i], NN)
            expo = jnp.exp2(scores * T_SCALE - offset[i : i + 1, :])
            out_ref[i] = (expo - wide).astype(BF16)

    return call(
        body,
        steps,
        [
            whole(feats.shape),
            whole(offset_packed.shape),
            pl.BlockSpec((half, width), lambda c: (2 * c, 0)),
            pl.BlockSpec((half, LANES), lambda c: (2 * c, 0)),
        ],
        [pl.BlockSpec((blocks, half, t_rows), lambda c: (0, c, 0))],
        [struct((blocks, columns // 2, t_rows), BF16)],
        [pltpu.VMEM((max(blocks, 8), t_rows), F32)],
        2 * columns * width * t_rows * blocks,
        columns * t_rows * blocks // 2,
        10 * 2**20,
    )(feats, offset_packed, wt, scale)[0]


def weight_grad(feats, offset_packed, inverse, wt, shared, scale, near, all_columns):
    blocks, width, t_rows = feats.shape
    columns = wt.shape[0]
    half = T_CHUNK // 2
    steps = columns // T_CHUNK
    tr = t_rows // LANES
    share = shared.shape[1] - 8

    def body(
        feat_ref, off_ref, inv_ref, wt_ref, sh_ref, scale_ref, near_ref,
        out_ref, offset, factor, g, g_sum,
    ):
        @pl.when(pl.program_id(0) == 0)
        def _():
            fill_offsets(offset, off_ref[...], blocks, tr)
            fill_offsets(factor, inv_ref[...], blocks, tr)
            total = jnp.zeros((8, LANES), F32)
            for i in range(blocks):
                high, low = halves(sh_ref[i, :share, :] * factor[i : i + 1, :] / STUDENT_TEMP)
                part = jnp.concatenate([high, low, jnp.zeros((LANES - 2 * share, t_rows), BF16)])
                g[i] = part
                total += mm(jnp.ones((8, t_rows), BF16), part, NT)
            g_sum[...] = total

        middle, wide = middle_of(scale_ref[...], all_columns, blocks * t_rows, tr)
        early = middle[:half] * g_sum[0:1, :]
        late = middle[half:] * g_sum[0:1, :]
        for i in range(blocks):
            scores = mm(wt_ref[...], feat_ref[i], NN)
            expo = jnp.exp2(scores * T_SCALE - offset[i : i + 1, :])
            late += mm((expo - wide[half:]).astype(BF16), g[i], NT)
            early += mm(near_ref[i], g[i], NT)
        out = (jnp.concatenate([early, late]) * scale_ref[...]).T
        out_ref[...] = out[:share] + out[share : 2 * share]

    return call(
        body,
        steps,
        [
            whole(feats.shape),
            whole(offset_packed.shape),
            whole(inverse.shape),
            pl.BlockSpec((half, width), lambda c: (2 * c + 1, 0)),
            whole(shared.shape),
            pl.BlockSpec((T_CHUNK, LANES), lambda c: (c, 0)),
            pl.BlockSpec((blocks, half, t_rows), lambda c: (0, c, 0)),
        ],
        [pl.BlockSpec((share, T_CHUNK), lambda c: (0, c))],
        [struct((share, columns))],
        [
            pltpu.VMEM((max(blocks, 8), t_rows), F32),
            pltpu.VMEM((max(blocks, 8), t_rows), F32),
            pltpu.VMEM((blocks, LANES, t_rows), BF16),
            pltpu.VMEM((8, LANES), F32),
        ],
        6 * columns * width * t_rows * blocks,
        columns * t_rows * blocks,
        14 * 2**20,
    )(feats, offset_packed, inverse, wt, shared, scale, near)[0]


def per_device(tf, sf, w, pairing):
    t_rows = tf.shape[0]
    rows = sf.shape[0]
    blocks = lax.axis_size("batch")
    peers = lax.axis_size("proto")
    me = lax.axis_index("batch").astype(jnp.int32).reshape(1)

    def swap(x, axis):
        return lax.all_to_all(x, axis, 0, 0)

    feats_f32 = lax.all_gather(turned(tf), "batch")
    pairs = pairing - me * t_rows
    onehot = (pairs[:, None] == jnp.arange(t_rows, dtype=jnp.int32)[None, :]).astype(BF16)
    gt = mm(sf, onehot, TN)
    wt, stats = student_stats(sf, tf, w, peers)
    stats = swap(stats, "proto")
    lse, shared = merge_stats(stats, gt, rows, blocks)
    shared = swap(shared, "batch")
    ds_prob, dw_prob = student_grads(sf, w, wt, lse, 0, None, peers)

    feats, offset, mass, dw_prob = first_iteration(feats_f32, shared, wt, dw_prob, peers)
    ds_prob, dw_prob = student_grads(sf, w, wt, lse, 1, (ds_prob, dw_prob), peers)
    for _ in range(ITERS - 2):
        mass = jnp.sum(swap(mass, "proto"), axis=0)
        offset, mass, dw_prob = next_iteration(feats, offset, mass, wt, dw_prob, peers)
    dw_prob = lax.psum_scatter(dw_prob, "batch", scatter_dimension=0, tiled=True)
    mass = jnp.sum(swap(mass, "proto"), axis=0)
    offset, scale, taught, mass = last_iteration(me, feats, offset, mass, w, wt, gt, peers)
    all_columns = w.shape[1] * peers
    near = early_expos(feats, offset, wt, scale, all_columns)
    mass = jnp.sum(swap(mass, "proto"), axis=0)
    loss, inverse, ds = after_iterations(
        me, mass, lse, taught, onehot, ds_prob, near, blocks
    )
    ds = swap(ds, "proto")
    far = 1
    while far < blocks:
        loss = loss + lax.ppermute(loss, "batch", [(i, i ^ far) for i in range(blocks)])
        far *= 2
    d_weight = dw_prob - weight_grad(
        feats, offset, inverse, wt, shared, scale, near, all_columns
    )
    return loss[0, 0] / (rows * blocks), jnp.sum(ds, axis=0), d_weight


def solution(mesh):
    placed = (P("batch", None), P("batch", None), P(None, "proto"), P("batch"))
    return jax.shard_map(
        per_device,
        mesh=mesh,
        in_specs=placed,
        out_specs=(P(), P(("batch", "proto"), None), P("batch", "proto")),
        check_vma=False,
    )
```

```python
import math

import jax
import jax.numpy as jnp
from jax import lax
from jax.experimental import pallas as pl
from jax.experimental.pallas import tpu as pltpu
from jax.sharding import PartitionSpec as P

ITERS = 3
LANES = 128
STATS_CHUNK = 1024
S_CHUNK = 512
T_CHUNK = 1024
TEACHER_TEMP = 0.07
STUDENT_TEMP = 0.1
LOG2E = math.log2(math.e)
T_SCALE = LOG2E / TEACHER_TEMP
S_SCALE = LOG2E / STUDENT_TEMP
F32 = jnp.float32
BF16 = jnp.bfloat16
NN = (((1,), (0,)), ((), ()))
NT = (((1,), (1,)), ((), ()))
TN = (((0,), (0,)), ((), ()))
VMEM_LIMIT = 56 * 1024 * 1024


def mm(a, b, dims):
    return lax.dot_general(a, b, dims, preferred_element_type=F32)


def halves(x):
    high = x.astype(BF16)
    return high, (x - high.astype(F32)).astype(BF16)


def by_sublane(x, combine):
    return combine(x.reshape(x.shape[0] // 8, 8, x.shape[1]), axis=0)


def whole(shape):
    return pl.BlockSpec(shape, lambda c: (0,) * len(shape))


def call(
    body, grid, in_specs, out_specs, out_shape, scratch, flops, transcendentals, size, aliases=None
):
    return pl.pallas_call(
        body,
        grid=(grid,),
        in_specs=in_specs,
        out_specs=out_specs,
        out_shape=out_shape,
        scratch_shapes=scratch,
        input_output_aliases=aliases or {},
        cost_estimate=pl.CostEstimate(
            flops=flops, transcendentals=transcendentals, bytes_accessed=size
        ),
        compiler_params=pltpu.CompilerParams(
            dimension_semantics=("arbitrary",), vmem_limit_bytes=VMEM_LIMIT
        ),
    )


def struct(shape, dtype=F32):
    return jax.ShapeDtypeStruct(shape, dtype)


def put_rows(ref, first, row):
    for i in range(row.shape[1] // LANES):
        ref[first + i : first + i + 1, :] = row[:, i * LANES : (i + 1) * LANES]


def turned(tf):
    def body(tf_ref, out_ref):
        out_ref[...] = tf_ref[...].astype(F32).T

    return call(
        body, 1, [whole(tf.shape)], [whole(tf.shape[::-1])], [struct(tf.shape[::-1])], [], 0, 0, 2**18
    )(tf)[0]


def student_stats(sf, tf, w, peers):
    rows, width = sf.shape
    t_rows = tf.shape[0]
    columns = w.shape[1]
    steps = columns // STATS_CHUNK
    s_rows, tr = rows // LANES, t_rows // LANES
    lines = -(-(2 * s_rows + tr) // 8) * 8

    def body(sf_ref, tf_ref, w_ref, wt_ref, out_ref, high, total, t_high, line):
        step = pl.program_id(0)

        @pl.when(step == 0)
        def _():
            high[...] = jnp.full_like(high, -3e38)
            total[...] = jnp.zeros_like(total)
            t_high[...] = jnp.full_like(t_high, -3e38)

        wt = w_ref[...].T
        wt_ref[...] = wt
        scores = mm(wt, sf_ref[...], NT)
        before = high[...]
        now = jnp.maximum(before, by_sublane(scores, jnp.max))
        high[...] = now
        groups = scores.reshape(STATS_CHUNK // 8, 8, rows)
        part = jnp.sum(jnp.exp2((groups - now[None]) * S_SCALE), axis=0)
        total[...] = total[...] * jnp.exp2((before - now) * S_SCALE) + part
        t_high[...] = jnp.maximum(t_high[...], by_sublane(mm(wt, tf_ref[...], NT), jnp.max))

        @pl.when(step == steps - 1)
        def _():
            best = jnp.max(high[...], axis=0, keepdims=True)
            summed = jnp.sum(
                total[...] * jnp.exp2((high[...] - best) * S_SCALE), axis=0, keepdims=True
            )
            line[...] = jnp.zeros_like(line)
            put_rows(line, 0, best)
            put_rows(line, s_rows, summed)
            put_rows(line, 2 * s_rows, jnp.max(t_high[...], axis=0, keepdims=True))
            out_ref[...] = jnp.broadcast_to(line[...][None], out_ref.shape)

    return call(
        body,
        steps,
        [
            whole(sf.shape),
            whole(tf.shape),
            pl.BlockSpec((width, STATS_CHUNK), lambda c: (0, c)),
        ],
        [
            pl.BlockSpec((STATS_CHUNK, width), lambda c: (c, 0)),
            whole((peers, lines, LANES)),
        ],
        [
            struct((columns, width), BF16),
            struct((peers, lines, LANES)),
        ],
        [
            pltpu.VMEM((8, rows), F32),
            pltpu.VMEM((8, rows), F32),
            pltpu.VMEM((8, t_rows), F32),
            pltpu.VMEM((lines, LANES), F32),
        ],
        2 * columns * width * (rows + t_rows),
        columns * rows,
        8 * 2**20,
    )(sf, tf, w)


def merge_stats(stats, gt, rows, batches):
    width, t_rows = gt.shape
    share = width // batches
    s_rows, tr = rows // LANES, t_rows // LANES

    def body(stats_ref, gt_ref, lse_ref, out_ref):
        highs = stats_ref[:, :s_rows, :]
        best = jnp.max(highs, axis=0)
        total = jnp.sum(
            stats_ref[:, s_rows : 2 * s_rows, :] * jnp.exp2((highs - best[None]) * S_SCALE), axis=0
        )
        lse_ref[...] = best * S_SCALE + jnp.log2(total)
        t_best = jnp.max(stats_ref[:, 2 * s_rows : 2 * s_rows + tr, :], axis=0) * T_SCALE
        row = jnp.concatenate([t_best[i : i + 1, :] for i in range(tr)], axis=1)
        for b in range(batches):
            out_ref[b, :share, :] = gt_ref[b * share : (b + 1) * share, :]
            out_ref[b, share:, :] = jnp.broadcast_to(row, (8, t_rows))

    return call(
        body,
        1,
        [whole(stats.shape), whole(gt.shape)],
        [whole((s_rows, LANES)), whole((batches, share + 8, t_rows))],
        [struct((s_rows, LANES)), struct((batches, share + 8, t_rows))],
        [],
        stats.size * 4,
        stats.size,
        2**21,
    )(stats, gt)


def student_grads(sf, w, wt, lse, half, before, peers):
    rows, width = sf.shape
    columns = w.shape[1]
    all_steps = columns // S_CHUNK
    cut = (5 * all_steps) // 8
    steps = all_steps - cut if half else cut
    first = half * cut
    s_rows = rows // LANES

    def body(sf_ref, w_ref, wt_ref, lse_ref, *rest):
        if half:
            _, old_ref, ds_ref, dw_ref, lse_row, sft, acc = rest
        else:
            ds_ref, dw_ref, lse_row, sft, acc = rest
        step = pl.program_id(0)

        @pl.when(step == 0)
        def _():
            for i in range(s_rows):
                lse_row[:, i * LANES : (i + 1) * LANES] = lse_ref[i : i + 1, :]
            sft[...] = sf_ref[...].T
            acc[...] = old_ref[...] if half else jnp.zeros_like(acc)

        scores = mm(wt_ref[...], sf_ref[...], NT)
        high, low = halves(jnp.exp2(scores * S_SCALE - lse_row[...]))
        acc[...] += mm(w_ref[...], high, NN) + mm(w_ref[...], low, NN)
        dw_ref[...] = (mm(sft[...], high, NT) + mm(sft[...], low, NT)) / STUDENT_TEMP

        @pl.when(step == steps - 1)
        def _():
            if half:
                ds_ref[...] = (acc[...].T / STUDENT_TEMP).reshape(ds_ref.shape)
            else:
                ds_ref[...] = acc[...]

    ds_shape = (peers, rows // peers, width) if half else (width, rows)
    in_specs = [
        whole(sf.shape),
        pl.BlockSpec((width, S_CHUNK), lambda c: (0, c + first)),
        pl.BlockSpec((S_CHUNK, width), lambda c: (c + first, 0)),
        whole(lse.shape),
    ]
    operands = [sf, w, wt, lse]
    if half:
        in_specs += [pl.BlockSpec(memory_space=pl.ANY), whole((width, rows))]
        operands += [before[1], before[0]]
    return call(
        body,
        steps,
        in_specs,
        [whole(ds_shape), pl.BlockSpec((width, S_CHUNK), lambda c: (0, c + first))],
        [struct(ds_shape), struct((width, columns))],
        [
            pltpu.VMEM((1, rows), F32),
            pltpu.VMEM((width, rows), BF16),
            pltpu.VMEM((width, rows), F32),
        ],
        16 * columns * width * rows * steps // all_steps,
        columns * rows // 2,
        6 * 2**20,
        {4: 1} if half else None,
    )(*operands)


def fill_offsets(offset, packed, blocks, per_block):
    for i in range(blocks):
        for j in range(per_block):
            line = i * per_block + j
            offset[i : i + 1, j * LANES : (j + 1) * LANES] = packed[line : line + 1, :]


def expos_and_scale(wt, feats, offset, expo, blocks, all_columns):
    partial = None
    for i in range(blocks):
        scores = mm(wt, feats[i], NN)
        values = jnp.exp2(scores * T_SCALE - offset[i : i + 1, :])
        expo[i] = values
        for j in range(values.shape[1] // LANES):
            piece = values[:, j * LANES : (j + 1) * LANES]
            partial = piece if partial is None else partial + piece
    return 1.0 / (all_columns * jnp.sum(partial, axis=1, keepdims=True))


def add_rows(expo, scale, mass, blocks):
    for i in range(blocks):
        mass[i] += by_sublane(expo[i] * scale, jnp.sum)


def put_mass(mass, line, blocks):
    for i in range(blocks):
        row = jnp.sum(mass[i], axis=0, keepdims=True)
        put_rows(line, i * (row.shape[1] // LANES), row)


def first_iteration(feats_f32, shared, wt, passed, peers):
    blocks, width, t_rows = feats_f32.shape
    columns = wt.shape[0]
    steps = columns // T_CHUNK
    tr = t_rows // LANES
    share = shared.shape[1] - 8

    def body(
        feat_ref, shared_ref, wt_ref, _,
        feat_out, off_out, out_ref, __, offset, expo, mass, line,
    ):
        step = pl.program_id(0)

        @pl.when(step == 0)
        def _():
            feat_out[...] = feat_ref[...].astype(BF16)
            for i in range(blocks):
                row = shared_ref[i, 0:1, :]
                offset[i : i + 1, :] = row
                put_rows(off_out, i * tr, row)
            mass[...] = jnp.zeros_like(mass)

        scale = expos_and_scale(wt_ref[...], feat_out, offset, expo, blocks, columns * peers)
        add_rows(expo, scale, mass, blocks)

        @pl.when(step == steps - 1)
        def _():
            put_mass(mass, line, blocks)
            out_ref[...] = jnp.broadcast_to(line[...][None], out_ref.shape)

    return call(
        body,
        steps,
        [
            whole(feats_f32.shape),
            pl.BlockSpec((blocks, 8, t_rows), lambda c: (0, share // 8, 0)),
            pl.BlockSpec((T_CHUNK, width), lambda c: (c, 0)),
            pl.BlockSpec(memory_space=pl.ANY),
        ],
        [
            whole(feats_f32.shape),
            whole((blocks * tr, LANES)),
            whole((peers, blocks * tr, LANES)),
            pl.BlockSpec(memory_space=pl.ANY),
        ],
        [
            struct(feats_f32.shape, BF16),
            struct((blocks * tr, LANES)),
            struct((peers, blocks * tr, LANES)),
            struct(passed.shape),
        ],
        [
            pltpu.VMEM((max(blocks, 8), t_rows), F32),
            pltpu.VMEM((blocks, T_CHUNK, t_rows), F32),
            pltpu.VMEM((blocks, 8, t_rows), F32),
            pltpu.VMEM((blocks * tr, LANES), F32),
        ],
        5 * columns * width * t_rows * blocks,
        columns * t_rows * blocks,
        5 * 2**20,
        {3: 3},
    )(feats_f32, shared, wt, passed)


def next_iteration(feats, old, received, wt, passed, peers):
    blocks, width, t_rows = feats.shape
    columns = wt.shape[0]
    steps = columns // T_CHUNK
    tr = t_rows // LANES
    total_t = blocks * t_rows

    def body(
        feat_ref, old_ref, recv_ref, wt_ref, _,
        off_out, out_ref, __, offset, expo, mass, line,
    ):
        step = pl.program_id(0)

        @pl.when(step == 0)
        def _():
            packed = old_ref[...] + jnp.log2(total_t * recv_ref[...])
            off_out[...] = packed
            fill_offsets(offset, packed, blocks, tr)
            mass[...] = jnp.zeros_like(mass)

        scale = expos_and_scale(wt_ref[...], feat_ref, offset, expo, blocks, columns * peers)
        add_rows(expo, scale, mass, blocks)

        @pl.when(step == steps - 1)
        def _():
            put_mass(mass, line, blocks)
            out_ref[...] = jnp.broadcast_to(line[...][None], out_ref.shape)

    return call(
        body,
        steps,
        [
            whole(feats.shape),
            whole(old.shape),
            whole(received.shape),
            pl.BlockSpec((T_CHUNK, width), lambda c: (c, 0)),
            pl.BlockSpec(memory_space=pl.ANY),
        ],
        [
            whole(old.shape),
            whole((peers, blocks * tr, LANES)),
            pl.BlockSpec(memory_space=pl.ANY),
        ],
        [struct(old.shape), struct((peers, blocks * tr, LANES)), struct(passed.shape)],
        [
            pltpu.VMEM((max(blocks, 8), t_rows), F32),
            pltpu.VMEM((blocks, T_CHUNK, t_rows), F32),
            pltpu.VMEM((blocks, 8, t_rows), F32),
            pltpu.VMEM((blocks * tr, LANES), F32),
        ],
        5 * columns * width * t_rows * blocks,
        columns * t_rows * blocks,
        4 * 2**20,
        {4: 2},
    )(feats, old, received, wt, passed)


def last_iteration(me, feats, old, received, w, wt, gt, peers):
    blocks, width, t_rows = feats.shape
    columns = wt.shape[0]
    steps = columns // T_CHUNK
    tr = t_rows // LANES
    total_t = blocks * t_rows
    lines = -(-(blocks * tr + tr) // 8) * 8

    def body(
        me_ref, feat_ref, old_ref, recv_ref, w_ref, wt_ref, gt_ref,
        off_out, scale_out, taught_ref, out_ref, offset, expo, mass, line, acc, w_last, high, low,
    ):
        step = pl.program_id(0)

        @pl.when(step == 0)
        def _():
            packed = old_ref[...] + jnp.log2(total_t * recv_ref[...])
            off_out[...] = packed
            fill_offsets(offset, packed, blocks, tr)
            mass[...] = jnp.zeros_like(mass)
            acc[...] = jnp.zeros_like(acc)
            w_last[...] = jnp.zeros_like(w_last)
            high[...] = jnp.zeros_like(high)
            low[...] = jnp.zeros_like(low)

        def add_taught():
            acc[...] += mm(w_last[...], high[...], NN) + mm(w_last[...], low[...], NN)

        scale = expos_and_scale(wt_ref[...], feat_ref, offset, expo, blocks, columns * peers)
        scale_out[...] = jnp.broadcast_to(scale, scale_out.shape)
        add_taught()
        add_rows(expo, scale, mass, blocks)
        high[...], low[...] = halves(expo[me_ref[0]] * scale)
        w_last[...] = w_ref[...]

        @pl.when(step == steps - 1)
        def _():
            add_taught()
            line[...] = jnp.zeros_like(line)
            put_mass(mass, line, blocks)
            put_rows(line, blocks * tr, jnp.sum(acc[...] * gt_ref[...], axis=0, keepdims=True))
            out_ref[...] = jnp.broadcast_to(line[...][None], out_ref.shape)
            taught_ref[...] = acc[...]

    return call(
        body,
        steps,
        [
            pl.BlockSpec(memory_space=pltpu.SMEM),
            whole(feats.shape),
            whole(old.shape),
            whole(received.shape),
            pl.BlockSpec((width, T_CHUNK), lambda c: (0, c)),
            pl.BlockSpec((T_CHUNK, width), lambda c: (c, 0)),
            whole(gt.shape),
        ],
        [
            whole(old.shape),
            pl.BlockSpec((T_CHUNK, LANES), lambda c: (c, 0)),
            whole((width, t_rows)),
            whole((peers, lines, LANES)),
        ],
        [
            struct(old.shape),
            struct((columns, LANES)),
            struct((width, t_rows)),
            struct((peers, lines, LANES)),
        ],
        [
            pltpu.VMEM((max(blocks, 8), t_rows), F32),
            pltpu.VMEM((blocks, T_CHUNK, t_rows), F32),
            pltpu.VMEM((blocks, 8, t_rows), F32),
            pltpu.VMEM((lines, LANES), F32),
            pltpu.VMEM((width, t_rows), F32),
            pltpu.VMEM((width, T_CHUNK), BF16),
            pltpu.VMEM((T_CHUNK, t_rows), BF16),
            pltpu.VMEM((T_CHUNK, t_rows), BF16),
        ],
        2 * columns * width * t_rows * (blocks + 2),
        columns * t_rows * blocks,
        8 * 2**20,
    )(me, feats, old, received, w, wt, gt)


def after_iterations(me, received, lse, taught, onehot, ds_prob, near, blocks):
    width, t_rows = taught.shape
    tr = t_rows // LANES
    n = blocks * tr

    def body(
        me_ref, recv_ref, lse_ref, taught_ref, oh_ref, prob_ref, _, part_ref, inv_ref, ds_ref
    ):
        inv_ref[...] = 1.0 / recv_ref[:n, :]
        inverse = inv_ref[pl.ds(me_ref[0] * tr, tr), :]
        product = jnp.sum(recv_ref[n : n + tr, :] * inverse) / STUDENT_TEMP
        part_ref[...] = jnp.full(part_ref.shape, jnp.sum(lse_ref[...]) / LOG2E - product, F32)
        row = jnp.concatenate([inverse[i : i + 1, :] for i in range(tr)], axis=1)
        high, low = halves(taught_ref[...] * row / STUDENT_TEMP)
        wanted = mm(oh_ref[...], high, NT) + mm(oh_ref[...], low, NT)
        ds_ref[...] = prob_ref[...] - wanted.reshape(ds_ref.shape)

    return call(
        body,
        1,
        [
            pl.BlockSpec(memory_space=pltpu.SMEM),
            whole(received.shape),
            whole(lse.shape),
            whole(taught.shape),
            whole(onehot.shape),
            whole(ds_prob.shape),
            pl.BlockSpec(memory_space=pl.ANY),
        ],
        [whole((8, LANES)), whole((n, LANES)), whole(ds_prob.shape)],
        [struct((8, LANES)), struct((n, LANES)), struct(ds_prob.shape)],
        [],
        4 * onehot.size * width,
        1024,
        3 * 2**20,
    )(me, received, lse, taught, onehot, ds_prob, near)


def middle_of(scale_ref, all_columns, total_t, tr):
    middle = 1.0 / (all_columns * total_t * scale_ref)
    return middle, jnp.concatenate([middle] * tr, axis=1)


def early_expos(feats, offset_packed, wt, scale, all_columns):
    blocks, width, t_rows = feats.shape
    columns = wt.shape[0]
    half = T_CHUNK // 2
    steps = columns // T_CHUNK
    tr = t_rows // LANES

    def body(feat_ref, off_ref, wt_ref, scale_ref, out_ref, offset):
        @pl.when(pl.program_id(0) == 0)
        def _():
            fill_offsets(offset, off_ref[...], blocks, tr)

        _, wide = middle_of(scale_ref[...], all_columns, blocks * t_rows, tr)
        for i in range(blocks):
            scores = mm(wt_ref[...], feat_ref[i], NN)
            expo = jnp.exp2(scores * T_SCALE - offset[i : i + 1, :])
            out_ref[i] = (expo - wide).astype(BF16)

    return call(
        body,
        steps,
        [
            whole(feats.shape),
            whole(offset_packed.shape),
            pl.BlockSpec((half, width), lambda c: (2 * c, 0)),
            pl.BlockSpec((half, LANES), lambda c: (2 * c, 0)),
        ],
        [pl.BlockSpec((blocks, half, t_rows), lambda c: (0, c, 0))],
        [struct((blocks, columns // 2, t_rows), BF16)],
        [pltpu.VMEM((max(blocks, 8), t_rows), F32)],
        2 * columns * width * t_rows * blocks,
        columns * t_rows * blocks // 2,
        10 * 2**20,
    )(feats, offset_packed, wt, scale)[0]


def weight_grad(feats, offset_packed, inverse, wt, shared, scale, near, all_columns):
    blocks, width, t_rows = feats.shape
    columns = wt.shape[0]
    half = T_CHUNK // 2
    steps = columns // T_CHUNK
    tr = t_rows // LANES
    share = shared.shape[1] - 8

    def body(
        feat_ref, off_ref, inv_ref, wt_ref, sh_ref, scale_ref, near_ref,
        out_ref, offset, factor, g, g_sum,
    ):
        @pl.when(pl.program_id(0) == 0)
        def _():
            fill_offsets(offset, off_ref[...], blocks, tr)
            fill_offsets(factor, inv_ref[...], blocks, tr)
            total = jnp.zeros((8, LANES), F32)
            for i in range(blocks):
                high, low = halves(sh_ref[i, :share, :] * factor[i : i + 1, :] / STUDENT_TEMP)
                part = jnp.concatenate([high, low, jnp.zeros((LANES - 2 * share, t_rows), BF16)])
                g[i] = part
                total += mm(jnp.ones((8, t_rows), BF16), part, NT)
            g_sum[...] = total

        middle, wide = middle_of(scale_ref[...], all_columns, blocks * t_rows, tr)
        early = middle[:half] * g_sum[0:1, :]
        late = middle[half:] * g_sum[0:1, :]
        for i in range(blocks):
            scores = mm(wt_ref[...], feat_ref[i], NN)
            expo = jnp.exp2(scores * T_SCALE - offset[i : i + 1, :])
            late += mm((expo - wide[half:]).astype(BF16), g[i], NT)
            early += mm(near_ref[i], g[i], NT)
        out = (jnp.concatenate([early, late]) * scale_ref[...]).T
        out_ref[...] = out[:share] + out[share : 2 * share]

    return call(
        body,
        steps,
        [
            whole(feats.shape),
            whole(offset_packed.shape),
            whole(inverse.shape),
            pl.BlockSpec((half, width), lambda c: (2 * c + 1, 0)),
            whole(shared.shape),
            pl.BlockSpec((T_CHUNK, LANES), lambda c: (c, 0)),
            pl.BlockSpec((blocks, half, t_rows), lambda c: (0, c, 0)),
        ],
        [pl.BlockSpec((share, T_CHUNK), lambda c: (0, c))],
        [struct((share, columns))],
        [
            pltpu.VMEM((max(blocks, 8), t_rows), F32),
            pltpu.VMEM((max(blocks, 8), t_rows), F32),
            pltpu.VMEM((blocks, LANES, t_rows), BF16),
            pltpu.VMEM((8, LANES), F32),
        ],
        6 * columns * width * t_rows * blocks,
        columns * t_rows * blocks,
        14 * 2**20,
    )(feats, offset_packed, inverse, wt, shared, scale, near)[0]


def per_device(tf, sf, w, pairing):
    t_rows = tf.shape[0]
    rows = sf.shape[0]
    blocks = lax.axis_size("batch")
    peers = lax.axis_size("proto")
    me = lax.axis_index("batch").astype(jnp.int32).reshape(1)

    def swap(x, axis):
        return lax.all_to_all(x, axis, 0, 0)

    feats_f32 = lax.all_gather(turned(tf), "batch")
    pairs = pairing - me * t_rows
    onehot = (pairs[:, None] == jnp.arange(t_rows, dtype=jnp.int32)[None, :]).astype(BF16)
    gt = mm(sf, onehot, TN)
    wt, stats = student_stats(sf, tf, w, peers)
    stats = swap(stats, "proto")
    lse, shared = merge_stats(stats, gt, rows, blocks)
    shared = swap(shared, "batch")
    ds_prob, dw_prob = student_grads(sf, w, wt, lse, 0, None, peers)

    feats, offset, mass, dw_prob = first_iteration(feats_f32, shared, wt, dw_prob, peers)
    ds_prob, dw_prob = student_grads(sf, w, wt, lse, 1, (ds_prob, dw_prob), peers)
    for _ in range(ITERS - 2):
        mass = jnp.sum(swap(mass, "proto"), axis=0)
        offset, mass, dw_prob = next_iteration(feats, offset, mass, wt, dw_prob, peers)
    dw_prob = lax.psum_scatter(dw_prob, "batch", scatter_dimension=0, tiled=True)
    mass = jnp.sum(swap(mass, "proto"), axis=0)
    offset, scale, taught, mass = last_iteration(me, feats, offset, mass, w, wt, gt, peers)
    all_columns = w.shape[1] * peers
    near = early_expos(feats, offset, wt, scale, all_columns)
    mass = jnp.sum(swap(mass, "proto"), axis=0)
    loss, inverse, ds = after_iterations(
        me, mass, lse, taught, onehot, ds_prob, near, blocks
    )
    ds = swap(ds, "proto")
    far = 1
    while far < blocks:
        loss = loss + lax.ppermute(loss, "batch", [(i, i ^ far) for i in range(blocks)])
        far *= 2
    d_weight = dw_prob - weight_grad(
        feats, offset, inverse, wt, shared, scale, near, all_columns
    )
    return loss[0, 0] / (rows * blocks), jnp.sum(ds, axis=0), d_weight


def solution(mesh):
    placed = (P("batch", None), P("batch", None), P(None, "proto"), P("batch"))
    return jax.shard_map(
        per_device,
        mesh=mesh,
        in_specs=placed,
        out_specs=(P(), P(("batch", "proto"), None), P("batch", "proto")),
        check_vma=False,
    )
```

```python
import math

import jax
import jax.numpy as jnp
from jax import lax
from jax.experimental import pallas as pl
from jax.experimental.pallas import tpu as pltpu
from jax.sharding import PartitionSpec as P

ITERS = 3
LANES = 128
STATS_CHUNK = 1024
S_CHUNK = 512
PASS_CHUNK = 2048
T_CHUNK = 1024
TEACHER_TEMP = 0.07
STUDENT_TEMP = 0.1
LOG2E = math.log2(math.e)
T_SCALE = LOG2E / TEACHER_TEMP
S_SCALE = LOG2E / STUDENT_TEMP
F32 = jnp.float32
BF16 = jnp.bfloat16
NN = (((1,), (0,)), ((), ()))
NT = (((1,), (1,)), ((), ()))
TN = (((0,), (0,)), ((), ()))
VMEM_LIMIT = 56 * 1024 * 1024


def mm(a, b, dims):
    return lax.dot_general(a, b, dims, preferred_element_type=F32)


def halves(x):
    high = x.astype(BF16)
    return high, (x - high.astype(F32)).astype(BF16)


def by_sublane(x, combine):
    return combine(x.reshape(x.shape[0] // 8, 8, x.shape[1]), axis=0)


def whole(shape):
    return pl.BlockSpec(shape, lambda c: (0,) * len(shape))


def call(
    body, grid, in_specs, out_specs, out_shape, scratch, flops, transcendentals, size, aliases=None
):
    return pl.pallas_call(
        body,
        grid=(grid,),
        in_specs=in_specs,
        out_specs=out_specs,
        out_shape=out_shape,
        scratch_shapes=scratch,
        input_output_aliases=aliases or {},
        cost_estimate=pl.CostEstimate(
            flops=flops, transcendentals=transcendentals, bytes_accessed=size
        ),
        compiler_params=pltpu.CompilerParams(
            dimension_semantics=("arbitrary",), vmem_limit_bytes=VMEM_LIMIT
        ),
    )


def struct(shape, dtype=F32):
    return jax.ShapeDtypeStruct(shape, dtype)


def put_rows(ref, first, row):
    for i in range(row.shape[1] // LANES):
        ref[first + i : first + i + 1, :] = row[:, i * LANES : (i + 1) * LANES]


def turned(tf):
    def body(tf_ref, out_ref):
        out_ref[...] = tf_ref[...].astype(F32).T

    return call(
        body, 1, [whole(tf.shape)], [whole(tf.shape[::-1])], [struct(tf.shape[::-1])], [], 0, 0, 2**18
    )(tf)[0]


def student_stats(sf, tf, w, peers):
    rows, width = sf.shape
    t_rows = tf.shape[0]
    columns = w.shape[1]
    steps = columns // STATS_CHUNK
    s_rows, tr = rows // LANES, t_rows // LANES
    lines = -(-(2 * s_rows + tr) // 8) * 8

    def body(sf_ref, tf_ref, w_ref, wt_ref, out_ref, high, total, t_high, line):
        step = pl.program_id(0)

        @pl.when(step == 0)
        def _():
            high[...] = jnp.full_like(high, -3e38)
            total[...] = jnp.zeros_like(total)
            t_high[...] = jnp.full_like(t_high, -3e38)

        wt = w_ref[...].T
        wt_ref[...] = wt
        scores = mm(wt, sf_ref[...], NT)
        before = high[...]
        now = jnp.maximum(before, by_sublane(scores, jnp.max))
        high[...] = now
        groups = scores.reshape(STATS_CHUNK // 8, 8, rows)
        part = jnp.sum(jnp.exp2((groups - now[None]) * S_SCALE), axis=0)
        total[...] = total[...] * jnp.exp2((before - now) * S_SCALE) + part
        t_high[...] = jnp.maximum(t_high[...], by_sublane(mm(wt, tf_ref[...], NT), jnp.max))

        @pl.when(step == steps - 1)
        def _():
            best = jnp.max(high[...], axis=0, keepdims=True)
            summed = jnp.sum(
                total[...] * jnp.exp2((high[...] - best) * S_SCALE), axis=0, keepdims=True
            )
            line[...] = jnp.zeros_like(line)
            put_rows(line, 0, best)
            put_rows(line, s_rows, summed)
            put_rows(line, 2 * s_rows, jnp.max(t_high[...], axis=0, keepdims=True))
            out_ref[...] = jnp.broadcast_to(line[...][None], out_ref.shape)

    return call(
        body,
        steps,
        [
            whole(sf.shape),
            whole(tf.shape),
            pl.BlockSpec((width, STATS_CHUNK), lambda c: (0, c)),
        ],
        [
            pl.BlockSpec((STATS_CHUNK, width), lambda c: (c, 0)),
            whole((peers, lines, LANES)),
        ],
        [
            struct((columns, width), BF16),
            struct((peers, lines, LANES)),
        ],
        [
            pltpu.VMEM((8, rows), F32),
            pltpu.VMEM((8, rows), F32),
            pltpu.VMEM((8, t_rows), F32),
            pltpu.VMEM((lines, LANES), F32),
        ],
        2 * columns * width * (rows + t_rows),
        columns * rows,
        8 * 2**20,
    )(sf, tf, w)


def merge_stats(stats, gt, rows, batches):
    width, t_rows = gt.shape
    share = width // batches
    s_rows, tr = rows // LANES, t_rows // LANES

    def body(stats_ref, gt_ref, lse_ref, out_ref):
        highs = stats_ref[:, :s_rows, :]
        best = jnp.max(highs, axis=0)
        total = jnp.sum(
            stats_ref[:, s_rows : 2 * s_rows, :] * jnp.exp2((highs - best[None]) * S_SCALE), axis=0
        )
        lse_ref[...] = best * S_SCALE + jnp.log2(total)
        t_best = jnp.max(stats_ref[:, 2 * s_rows : 2 * s_rows + tr, :], axis=0) * T_SCALE
        row = jnp.concatenate([t_best[i : i + 1, :] for i in range(tr)], axis=1)
        for b in range(batches):
            out_ref[b, :share, :] = gt_ref[b * share : (b + 1) * share, :]
            out_ref[b, share:, :] = jnp.broadcast_to(row, (8, t_rows))

    return call(
        body,
        1,
        [whole(stats.shape), whole(gt.shape)],
        [whole((s_rows, LANES)), whole((batches, share + 8, t_rows))],
        [struct((s_rows, LANES)), struct((batches, share + 8, t_rows))],
        [],
        stats.size * 4,
        stats.size,
        2**21,
    )(stats, gt)


def student_grads(sf, w, wt, lse, half, before, peers):
    rows, width = sf.shape
    columns = w.shape[1]
    all_steps = columns // S_CHUNK
    cut = (5 * all_steps) // 8
    steps = all_steps - cut if half else cut
    first = half * cut
    s_rows = rows // LANES

    def body(sf_ref, w_ref, wt_ref, lse_ref, *rest):
        if half:
            _, old_ref, ds_ref, dw_ref, lse_row, sft, acc = rest
        else:
            ds_ref, dw_ref, lse_row, sft, acc = rest
        step = pl.program_id(0)

        @pl.when(step == 0)
        def _():
            for i in range(s_rows):
                lse_row[:, i * LANES : (i + 1) * LANES] = lse_ref[i : i + 1, :]
            sft[...] = sf_ref[...].T
            acc[...] = old_ref[...] if half else jnp.zeros_like(acc)

        scores = mm(wt_ref[...], sf_ref[...], NT)
        high, low = halves(jnp.exp2(scores * S_SCALE - lse_row[...]))
        acc[...] += mm(w_ref[...], high, NN) + mm(w_ref[...], low, NN)
        dw_ref[...] = (mm(sft[...], high, NT) + mm(sft[...], low, NT)) / STUDENT_TEMP

        @pl.when(step == steps - 1)
        def _():
            if half:
                ds_ref[...] = (acc[...].T / STUDENT_TEMP).reshape(ds_ref.shape)
            else:
                ds_ref[...] = acc[...]

    ds_shape = (peers, rows // peers, width) if half else (width, rows)
    in_specs = [
        whole(sf.shape),
        pl.BlockSpec((width, S_CHUNK), lambda c: (0, c + first)),
        pl.BlockSpec((S_CHUNK, width), lambda c: (c + first, 0)),
        whole(lse.shape),
    ]
    operands = [sf, w, wt, lse]
    if half:
        in_specs += [pl.BlockSpec(memory_space=pl.ANY), whole((width, rows))]
        operands += [before[1], before[0]]
    return call(
        body,
        steps,
        in_specs,
        [whole(ds_shape), pl.BlockSpec((width, S_CHUNK), lambda c: (0, c + first))],
        [struct(ds_shape), struct((width, columns))],
        [
            pltpu.VMEM((1, rows), F32),
            pltpu.VMEM((width, rows), BF16),
            pltpu.VMEM((width, rows), F32),
        ],
        16 * columns * width * rows * steps // all_steps,
        columns * rows // 2,
        6 * 2**20,
        {4: 1} if half else None,
    )(*operands)


def fill_offsets(offset, packed, blocks, per_block):
    for i in range(blocks):
        for j in range(per_block):
            line = i * per_block + j
            offset[i : i + 1, j * LANES : (j + 1) * LANES] = packed[line : line + 1, :]


def expos_and_scale(wt, feats, offset, expo, blocks, all_columns):
    partial = None
    for i in range(blocks):
        scores = mm(wt, feats[i], NN)
        values = jnp.exp2(scores * T_SCALE - offset[i : i + 1, :])
        expo[i] = values
        for j in range(values.shape[1] // LANES):
            piece = values[:, j * LANES : (j + 1) * LANES]
            partial = piece if partial is None else partial + piece
    return 1.0 / (all_columns * jnp.sum(partial, axis=1, keepdims=True))


def add_rows(expo, scale, mass, blocks):
    for i in range(blocks):
        mass[i] += by_sublane(expo[i] * scale, jnp.sum)


def put_mass(mass, line, blocks):
    for i in range(blocks):
        row = jnp.sum(mass[i], axis=0, keepdims=True)
        put_rows(line, i * (row.shape[1] // LANES), row)


def first_iteration(feats_f32, shared, wt, passed, peers):
    blocks, width, t_rows = feats_f32.shape
    columns = wt.shape[0]
    steps = columns // PASS_CHUNK
    tr = t_rows // LANES
    share = shared.shape[1] - 8

    def body(
        feat_ref, shared_ref, wt_ref, _,
        feat_out, off_out, out_ref, __, offset, expo, mass, line,
    ):
        step = pl.program_id(0)

        @pl.when(step == 0)
        def _():
            feat_out[...] = feat_ref[...].astype(BF16)
            for i in range(blocks):
                row = shared_ref[i, 0:1, :]
                offset[i : i + 1, :] = row
                put_rows(off_out, i * tr, row)
            mass[...] = jnp.zeros_like(mass)

        scale = expos_and_scale(wt_ref[...], feat_out, offset, expo, blocks, columns * peers)
        add_rows(expo, scale, mass, blocks)

        @pl.when(step == steps - 1)
        def _():
            put_mass(mass, line, blocks)
            out_ref[...] = jnp.broadcast_to(line[...][None], out_ref.shape)

    return call(
        body,
        steps,
        [
            whole(feats_f32.shape),
            pl.BlockSpec((blocks, 8, t_rows), lambda c: (0, share // 8, 0)),
            pl.BlockSpec((PASS_CHUNK, width), lambda c: (c, 0)),
            pl.BlockSpec(memory_space=pl.ANY),
        ],
        [
            whole(feats_f32.shape),
            whole((blocks * tr, LANES)),
            whole((peers, blocks * tr, LANES)),
            pl.BlockSpec(memory_space=pl.ANY),
        ],
        [
            struct(feats_f32.shape, BF16),
            struct((blocks * tr, LANES)),
            struct((peers, blocks * tr, LANES)),
            struct(passed.shape),
        ],
        [
            pltpu.VMEM((max(blocks, 8), t_rows), F32),
            pltpu.VMEM((blocks, PASS_CHUNK, t_rows), F32),
            pltpu.VMEM((blocks, 8, t_rows), F32),
            pltpu.VMEM((blocks * tr, LANES), F32),
        ],
        5 * columns * width * t_rows * blocks,
        columns * t_rows * blocks,
        5 * 2**20,
        {3: 3},
    )(feats_f32, shared, wt, passed)


def next_iteration(feats, old, received, wt, passed, peers):
    blocks, width, t_rows = feats.shape
    columns = wt.shape[0]
    steps = columns // PASS_CHUNK
    tr = t_rows // LANES
    total_t = blocks * t_rows

    def body(
        feat_ref, old_ref, recv_ref, wt_ref, _,
        off_out, out_ref, __, offset, expo, mass, line,
    ):
        step = pl.program_id(0)

        @pl.when(step == 0)
        def _():
            packed = old_ref[...] + jnp.log2(total_t * recv_ref[...])
            off_out[...] = packed
            fill_offsets(offset, packed, blocks, tr)
            mass[...] = jnp.zeros_like(mass)

        scale = expos_and_scale(wt_ref[...], feat_ref, offset, expo, blocks, columns * peers)
        add_rows(expo, scale, mass, blocks)

        @pl.when(step == steps - 1)
        def _():
            put_mass(mass, line, blocks)
            out_ref[...] = jnp.broadcast_to(line[...][None], out_ref.shape)

    return call(
        body,
        steps,
        [
            whole(feats.shape),
            whole(old.shape),
            whole(received.shape),
            pl.BlockSpec((PASS_CHUNK, width), lambda c: (c, 0)),
            pl.BlockSpec(memory_space=pl.ANY),
        ],
        [
            whole(old.shape),
            whole((peers, blocks * tr, LANES)),
            pl.BlockSpec(memory_space=pl.ANY),
        ],
        [struct(old.shape), struct((peers, blocks * tr, LANES)), struct(passed.shape)],
        [
            pltpu.VMEM((max(blocks, 8), t_rows), F32),
            pltpu.VMEM((blocks, PASS_CHUNK, t_rows), F32),
            pltpu.VMEM((blocks, 8, t_rows), F32),
            pltpu.VMEM((blocks * tr, LANES), F32),
        ],
        5 * columns * width * t_rows * blocks,
        columns * t_rows * blocks,
        4 * 2**20,
        {4: 2},
    )(feats, old, received, wt, passed)


def last_iteration(me, feats, old, received, w, wt, gt, peers):
    blocks, width, t_rows = feats.shape
    columns = wt.shape[0]
    steps = columns // PASS_CHUNK
    tr = t_rows // LANES
    total_t = blocks * t_rows
    lines = -(-(blocks * tr + tr) // 8) * 8

    def body(
        me_ref, feat_ref, old_ref, recv_ref, w_ref, wt_ref, gt_ref,
        off_out, scale_out, taught_ref, out_ref, offset, expo, mass, line, acc, w_last, high, low,
    ):
        step = pl.program_id(0)

        @pl.when(step == 0)
        def _():
            packed = old_ref[...] + jnp.log2(total_t * recv_ref[...])
            off_out[...] = packed
            fill_offsets(offset, packed, blocks, tr)
            mass[...] = jnp.zeros_like(mass)
            acc[...] = jnp.zeros_like(acc)
            w_last[...] = jnp.zeros_like(w_last)
            high[...] = jnp.zeros_like(high)
            low[...] = jnp.zeros_like(low)

        def add_taught():
            acc[...] += mm(w_last[...], high[...], NN) + mm(w_last[...], low[...], NN)

        scale = expos_and_scale(wt_ref[...], feat_ref, offset, expo, blocks, columns * peers)
        scale_out[...] = jnp.broadcast_to(scale, scale_out.shape)
        add_taught()
        add_rows(expo, scale, mass, blocks)
        high[...], low[...] = halves(expo[me_ref[0]] * scale)
        w_last[...] = w_ref[...]

        @pl.when(step == steps - 1)
        def _():
            add_taught()
            line[...] = jnp.zeros_like(line)
            put_mass(mass, line, blocks)
            put_rows(line, blocks * tr, jnp.sum(acc[...] * gt_ref[...], axis=0, keepdims=True))
            out_ref[...] = jnp.broadcast_to(line[...][None], out_ref.shape)
            taught_ref[...] = acc[...]

    return call(
        body,
        steps,
        [
            pl.BlockSpec(memory_space=pltpu.SMEM),
            whole(feats.shape),
            whole(old.shape),
            whole(received.shape),
            pl.BlockSpec((width, PASS_CHUNK), lambda c: (0, c)),
            pl.BlockSpec((PASS_CHUNK, width), lambda c: (c, 0)),
            whole(gt.shape),
        ],
        [
            whole(old.shape),
            pl.BlockSpec((PASS_CHUNK, LANES), lambda c: (c, 0)),
            whole((width, t_rows)),
            whole((peers, lines, LANES)),
        ],
        [
            struct(old.shape),
            struct((columns, LANES)),
            struct((width, t_rows)),
            struct((peers, lines, LANES)),
        ],
        [
            pltpu.VMEM((max(blocks, 8), t_rows), F32),
            pltpu.VMEM((blocks, PASS_CHUNK, t_rows), F32),
            pltpu.VMEM((blocks, 8, t_rows), F32),
            pltpu.VMEM((lines, LANES), F32),
            pltpu.VMEM((width, t_rows), F32),
            pltpu.VMEM((width, PASS_CHUNK), BF16),
            pltpu.VMEM((PASS_CHUNK, t_rows), BF16),
            pltpu.VMEM((PASS_CHUNK, t_rows), BF16),
        ],
        2 * columns * width * t_rows * (blocks + 2),
        columns * t_rows * blocks,
        8 * 2**20,
    )(me, feats, old, received, w, wt, gt)


def after_iterations(me, received, lse, taught, onehot, ds_prob, near, blocks):
    width, t_rows = taught.shape
    tr = t_rows // LANES
    n = blocks * tr

    def body(
        me_ref, recv_ref, lse_ref, taught_ref, oh_ref, prob_ref, _, part_ref, inv_ref, ds_ref
    ):
        inv_ref[...] = 1.0 / recv_ref[:n, :]
        inverse = inv_ref[pl.ds(me_ref[0] * tr, tr), :]
        product = jnp.sum(recv_ref[n : n + tr, :] * inverse) / STUDENT_TEMP
        part_ref[...] = jnp.full(part_ref.shape, jnp.sum(lse_ref[...]) / LOG2E - product, F32)
        row = jnp.concatenate([inverse[i : i + 1, :] for i in range(tr)], axis=1)
        high, low = halves(taught_ref[...] * row / STUDENT_TEMP)
        wanted = mm(oh_ref[...], high, NT) + mm(oh_ref[...], low, NT)
        ds_ref[...] = prob_ref[...] - wanted.reshape(ds_ref.shape)

    return call(
        body,
        1,
        [
            pl.BlockSpec(memory_space=pltpu.SMEM),
            whole(received.shape),
            whole(lse.shape),
            whole(taught.shape),
            whole(onehot.shape),
            whole(ds_prob.shape),
            pl.BlockSpec(memory_space=pl.ANY),
        ],
        [whole((8, LANES)), whole((n, LANES)), whole(ds_prob.shape)],
        [struct((8, LANES)), struct((n, LANES)), struct(ds_prob.shape)],
        [],
        4 * onehot.size * width,
        1024,
        3 * 2**20,
    )(me, received, lse, taught, onehot, ds_prob, near)


def middle_of(scale_ref, all_columns, total_t, tr):
    middle = 1.0 / (all_columns * total_t * scale_ref)
    return middle, jnp.concatenate([middle] * tr, axis=1)


def early_expos(feats, offset_packed, wt, scale, all_columns):
    blocks, width, t_rows = feats.shape
    columns = wt.shape[0]
    half = T_CHUNK // 2
    steps = columns // T_CHUNK
    tr = t_rows // LANES

    def body(feat_ref, off_ref, wt_ref, scale_ref, out_ref, offset):
        @pl.when(pl.program_id(0) == 0)
        def _():
            fill_offsets(offset, off_ref[...], blocks, tr)

        _, wide = middle_of(scale_ref[...], all_columns, blocks * t_rows, tr)
        for i in range(blocks):
            scores = mm(wt_ref[...], feat_ref[i], NN)
            expo = jnp.exp2(scores * T_SCALE - offset[i : i + 1, :])
            out_ref[i] = (expo - wide).astype(BF16)

    return call(
        body,
        steps,
        [
            whole(feats.shape),
            whole(offset_packed.shape),
            pl.BlockSpec((half, width), lambda c: (2 * c, 0)),
            pl.BlockSpec((half, LANES), lambda c: (2 * c, 0)),
        ],
        [pl.BlockSpec((blocks, half, t_rows), lambda c: (0, c, 0))],
        [struct((blocks, columns // 2, t_rows), BF16)],
        [pltpu.VMEM((max(blocks, 8), t_rows), F32)],
        2 * columns * width * t_rows * blocks,
        columns * t_rows * blocks // 2,
        10 * 2**20,
    )(feats, offset_packed, wt, scale)[0]


def weight_grad(feats, offset_packed, inverse, wt, shared, scale, near, all_columns):
    blocks, width, t_rows = feats.shape
    columns = wt.shape[0]
    half = T_CHUNK // 2
    steps = columns // T_CHUNK
    tr = t_rows // LANES
    share = shared.shape[1] - 8

    def body(
        feat_ref, off_ref, inv_ref, wt_ref, sh_ref, scale_ref, near_ref,
        out_ref, offset, factor, g, g_sum,
    ):
        @pl.when(pl.program_id(0) == 0)
        def _():
            fill_offsets(offset, off_ref[...], blocks, tr)
            fill_offsets(factor, inv_ref[...], blocks, tr)
            total = jnp.zeros((8, LANES), F32)
            for i in range(blocks):
                high, low = halves(sh_ref[i, :share, :] * factor[i : i + 1, :] / STUDENT_TEMP)
                part = jnp.concatenate([high, low, jnp.zeros((LANES - 2 * share, t_rows), BF16)])
                g[i] = part
                total += mm(jnp.ones((8, t_rows), BF16), part, NT)
            g_sum[...] = total

        middle, wide = middle_of(scale_ref[...], all_columns, blocks * t_rows, tr)
        early = middle[:half] * g_sum[0:1, :]
        late = middle[half:] * g_sum[0:1, :]
        for i in range(blocks):
            scores = mm(wt_ref[...], feat_ref[i], NN)
            expo = jnp.exp2(scores * T_SCALE - offset[i : i + 1, :])
            late += mm((expo - wide[half:]).astype(BF16), g[i], NT)
            early += mm(near_ref[i], g[i], NT)
        out = (jnp.concatenate([early, late]) * scale_ref[...]).T
        out_ref[...] = out[:share] + out[share : 2 * share]

    return call(
        body,
        steps,
        [
            whole(feats.shape),
            whole(offset_packed.shape),
            whole(inverse.shape),
            pl.BlockSpec((half, width), lambda c: (2 * c + 1, 0)),
            whole(shared.shape),
            pl.BlockSpec((T_CHUNK, LANES), lambda c: (c, 0)),
            pl.BlockSpec((blocks, half, t_rows), lambda c: (0, c, 0)),
        ],
        [pl.BlockSpec((share, T_CHUNK), lambda c: (0, c))],
        [struct((share, columns))],
        [
            pltpu.VMEM((max(blocks, 8), t_rows), F32),
            pltpu.VMEM((max(blocks, 8), t_rows), F32),
            pltpu.VMEM((blocks, LANES, t_rows), BF16),
            pltpu.VMEM((8, LANES), F32),
        ],
        6 * columns * width * t_rows * blocks,
        columns * t_rows * blocks,
        14 * 2**20,
    )(feats, offset_packed, inverse, wt, shared, scale, near)[0]


def per_device(tf, sf, w, pairing):
    t_rows = tf.shape[0]
    rows = sf.shape[0]
    blocks = lax.axis_size("batch")
    peers = lax.axis_size("proto")
    me = lax.axis_index("batch").astype(jnp.int32).reshape(1)

    def swap(x, axis):
        return lax.all_to_all(x, axis, 0, 0)

    feats_f32 = lax.all_gather(turned(tf), "batch")
    pairs = pairing - me * t_rows
    onehot = (pairs[:, None] == jnp.arange(t_rows, dtype=jnp.int32)[None, :]).astype(BF16)
    gt = mm(sf, onehot, TN)
    wt, stats = student_stats(sf, tf, w, peers)
    stats = swap(stats, "proto")
    lse, shared = merge_stats(stats, gt, rows, blocks)
    shared = swap(shared, "batch")
    ds_prob, dw_prob = student_grads(sf, w, wt, lse, 0, None, peers)

    feats, offset, mass, dw_prob = first_iteration(feats_f32, shared, wt, dw_prob, peers)
    ds_prob, dw_prob = student_grads(sf, w, wt, lse, 1, (ds_prob, dw_prob), peers)
    for _ in range(ITERS - 2):
        mass = jnp.sum(swap(mass, "proto"), axis=0)
        offset, mass, dw_prob = next_iteration(feats, offset, mass, wt, dw_prob, peers)
    dw_prob = lax.psum_scatter(dw_prob, "batch", scatter_dimension=0, tiled=True)
    mass = jnp.sum(swap(mass, "proto"), axis=0)
    offset, scale, taught, mass = last_iteration(me, feats, offset, mass, w, wt, gt, peers)
    all_columns = w.shape[1] * peers
    near = early_expos(feats, offset, wt, scale, all_columns)
    mass = jnp.sum(swap(mass, "proto"), axis=0)
    loss, inverse, ds = after_iterations(
        me, mass, lse, taught, onehot, ds_prob, near, blocks
    )
    ds = swap(ds, "proto")
    far = 1
    while far < blocks:
        loss = loss + lax.ppermute(loss, "batch", [(i, i ^ far) for i in range(blocks)])
        far *= 2
    d_weight = dw_prob - weight_grad(
        feats, offset, inverse, wt, shared, scale, near, all_columns
    )
    return loss[0, 0] / (rows * blocks), jnp.sum(ds, axis=0), d_weight


def solution(mesh):
    placed = (P("batch", None), P("batch", None), P(None, "proto"), P("batch"))
    return jax.shard_map(
        per_device,
        mesh=mesh,
        in_specs=placed,
        out_specs=(P(), P(("batch", "proto"), None), P("batch", "proto")),
        check_vma=False,
    )
```
